32 devices in a mesh: group: 2 (over y), ctx: 2 (over x), exp: 8 (over z, core).
Axes of the slice: x: 2, y: 2, z: 4, core: 2. Of those that a mesh axis runs over, the one named last changes fastest.
Arguments:
- queries: bfloat16 [1024, 2048], P(('group', 'ctx'), 'exp'), parts along dimension 0, may hold values from -80 to 80
- keys: bfloat16 [1024, 2048], P(('group', 'ctx'), 'exp'), parts along dimension 0, may hold values from -4 to 4
- values: bfloat16 [1024, 2048], P(('group', 'ctx'), 'exp'), parts along dimension 0, may hold values from -6 to 6
- out_weight: bfloat16 [2048, 2048], P('exp'), may hold values from -0.125 to 0.125
- residual_in: bfloat16 [1024, 2048], P(('group', 'ctx', 'exp')), parts along dimension 0, may hold values from -6 to 6
- gate_weight: bfloat16 [8, 2048, 704], P('exp', 'ctx'), may hold values from -0.125 to 0.125
- up_weight: bfloat16 [8, 2048, 704], P('exp', 'ctx'), may hold values from -0.125 to 0.125
- down_weight: bfloat16 [8, 704, 2048], P('exp', None, 'ctx'), may hold values from -0.21875 to 0.21875
- expert_ids: int32 [1024, 2], P(('group', 'ctx', 'exp')), parts along dimension 0, may hold values from 0 to 7, all different within a row; in each aligned block of 32 rows (0 to 31, 32 to 63, ...) at most 16 rows name the same one
- route_gates: float32 [1024, 2], P(('group', 'ctx', 'exp')), parts along dimension 0, may hold values from 0.2 to 1
Outputs:
- mixed: bfloat16 [1024, 2048], P(('group', 'ctx', 'exp')), parts along dimension 0
The draws below stay inside these ranges and needn't reach their ends.
There are 2 independent parts, one for each index of `group`. The reference program is written for one: setup_inputs(seed, part) draws one part's arguments, and reference() takes and returns one part's arrays. A program takes and returns all parts, laid end to end along the dimension named above; an argument that names none is the same for every part. Nothing has to cross between parts.
Inputs may be any that keep to these rules, and one draw needn't show every extreme that they name: `expert_ids`: in each aligned block of 32 rows (the rows of one device), no expert is named more than 16 times; the two experts of a row differ.
All inputs are finite; a program needn't handle non-finite values.
Results may differ from the reference program's by a relative error of at most 0.012.
Values may be sent and summed in bfloat16 or wider, within the bound.
A program may use at most 128 MiB of HBM per device.

```python
import math
import jax
import jax.numpy as jnp
import numpy as np
from jax import lax

D = 2048
HEAD_DIM = 128
HIDDEN_UNITS = 704
CAP = 16
TOKENS = 512
HEADS = 16
EXPERTS = 8
ROWS_DEV = 32


def base_keys(key):
    return jnp.clip(jax.random.normal(key, (TOKENS, HEADS * HEAD_DIM), jnp.float32), -4.0, 4.0)


def draw_keys(key, part):
    base = base_keys(key)
    return base.astype(jnp.bfloat16)


def draw_queries(key, part):
    base = base_keys(key)
    key = jax.random.fold_in(key, 7)
    own_key, first_key, second_key = jax.random.split(key, 3)
    own = jnp.clip(jax.random.normal(own_key, base.shape, jnp.float32), -4.0, 4.0)
    first = jax.random.randint(first_key, (TOKENS,), 0, TOKENS)
    second = jax.random.randint(second_key, (TOKENS,), 0, TOKENS)
    pair_weight = (math.log(TOKENS) + 2.0) / math.sqrt(HEAD_DIM)
    result = pair_weight * (base[first] + base[second]) + 0.5 * own
    return result.astype(jnp.bfloat16)


def block_scale(key, shape, shards, smallest, top_value):
    def one(position, parts):
        steps = jax.random.uniform(jax.random.fold_in(jax.random.fold_in(key, 6), position), (parts,), jnp.float32, smallest / len(shards), top_value / len(shards))
        return jnp.repeat(jnp.exp(steps), shape[position] // parts).reshape((-1,) + (1,) * (len(shape) - position - 1))

    factor_of = one(*shards[0])
    for cut in shards[1:]:
        factor_of = factor_of * one(*cut)
    return factor_of


def shared_out(key, own, number, rows, count, top, reach, skew):
    ranking = jax.random.permutation(key, count)
    crowded, usual = shares(count, rows * top, reach, skew, True), shares(count, rows * top, reach, skew, False)
    places = jnp.arange(count)

    def named(sizes, offset_by):
        used = int((sizes > 0).sum())
        fixed = max(1, used // 4)
        passed = fixed + (places - fixed + offset_by * (used - fixed)) % max(1, count - fixed)
        return jnp.zeros((count,), jnp.int32).at[ranking[jnp.where(places < fixed, places, passed)]].set(jnp.asarray(sizes, jnp.int32))

    sizes = jnp.where(number % 4 == 0, named(crowded, number // 4), named(usual, number - number // 4 - 1))
    mixed = jax.random.permutation(jax.random.fold_in(own, 3), count)
    source_of, sink = mixed[0:count // 2 * 2:2], mixed[1:count // 2 * 2:2]
    margin = jnp.minimum(sizes[source_of] - 1, reach - sizes[sink]) // 2
    margin = jnp.where((source_of == ranking[0]) | (sink == ranking[0]) | (sizes[sink] == 0), 0, jnp.maximum(margin, 0))
    passed = jax.random.randint(jax.random.fold_in(own, 4), (count // 2,), 0, 1 << 20) % (margin + 1)
    sizes = sizes.at[source_of].add(-passed).at[sink].add(passed)
    labels = jnp.searchsorted(jnp.cumsum(sizes), jnp.arange(rows * top), side="right").astype(jnp.int32)
    table = labels.reshape(top, rows).T
    table = table[jax.random.permutation(jax.random.fold_in(own, 1), rows)]
    offset_by = jax.random.randint(jax.random.fold_in(own, 2), (rows, 1), 0, top)
    return jnp.take_along_axis(table, (jnp.arange(top)[None, :] + offset_by) % top, axis=1)


def shares(amount, total, reach, lean, full):
    weights = [(1 << 20) // math.isqrt(rank ** lean) + 1 for rank in range(1, amount + 1)]
    largest = reach if full else min(reach, max(-(-total // amount), total * weights[0] // sum(weights)))
    least = 1 if total - largest >= amount - 1 else 0
    counts, spare = [largest] + [least] * (amount - 1), total - largest - least * (amount - 1)
    while spare > 0:
        free = [i for i in range(1, amount) if counts[i] < largest] or [i for i in range(1, amount) if counts[i] < reach]
        pool, left = sum([weights[i] for i in free]), spare
        for i in free:
            addition = min(reach - counts[i], max(1, left * weights[i] // pool), spare)
            counts[i] = counts[i] + addition
            spare = spare - addition
    return np.array(counts)


def bell_draw(rng, extent, scale, most, shards=(), held_as=jnp.bfloat16):
    entries = scale * jax.random.normal(rng, extent, jnp.float32)
    if shards:
        entries = entries * block_scale(rng, extent, shards, -0.22, 0.18)
    return jnp.clip(entries, -most, most).astype(held_as)


def setup_inputs(seed: int = 0, part: int = 0) -> dict:
    seeds = jax.random.split(jax.random.key(seed), 11)
    part_splits = jax.random.split(jax.random.fold_in(seeds[10], part), 11)
    queries = draw_queries(jax.random.fold_in(jax.random.fold_in(seeds[10], part), 71), part)
    keys = draw_keys(jax.random.fold_in(jax.random.fold_in(seeds[10], part), 71), part)
    values = bell_draw(part_splits[2], (TOKENS, HEADS * HEAD_DIM), 1.0, 6.0, ((0, 2), (1, 8)))
    out_weight = bell_draw(seeds[3], (HEADS * HEAD_DIM, D), (HEADS * HEAD_DIM) ** -0.5, 0.125, ((0, 8),))
    residual_in = bell_draw(part_splits[4], (TOKENS, D), 1.0, 6.0, ((0, 16),))
    gate_weight = bell_draw(seeds[5], (EXPERTS, D, HIDDEN_UNITS), D ** -0.5, 0.125, ((0, 8), (1, 2)))
    up_weight = bell_draw(seeds[6], (EXPERTS, D, HIDDEN_UNITS), D ** -0.5, 0.125, ((0, 8), (1, 2)))
    down_weight = bell_draw(seeds[7], (EXPERTS, HIDDEN_UNITS, D), HIDDEN_UNITS ** -0.5, 0.21875, ((0, 8), (2, 2)))
    expert_ids_keys = jax.random.split(jax.random.fold_in(part_splits[8], 1), TOKENS // ROWS_DEV)
    expert_ids_turns = jax.random.permutation(jax.random.fold_in(part_splits[8], 3), TOKENS // ROWS_DEV)
    expert_ids = jax.vmap(lambda own, number: shared_out(jax.random.fold_in(part_splits[8], 2), own, number, ROWS_DEV, EXPERTS, 2, CAP, 2))(expert_ids_keys, expert_ids_turns).reshape((TOKENS, 2))
    route_gates = jnp.clip(jnp.exp(math.log(1.0) - 1.609438 * jax.random.uniform(part_splits[9], (TOKENS, 2), jnp.float32) ** block_scale(part_splits[9], (TOKENS, 2), ((0, 16),), -0.2, 0.2)), 0.2, 1.0)
    return dict(queries=queries, keys=keys, values=values, out_weight=out_weight, residual_in=residual_in, gate_weight=gate_weight, up_weight=up_weight, down_weight=down_weight, expert_ids=expert_ids, route_gates=route_gates)


def expert_apply(index, slab, gate_weight, up_weight, down_weight):
    gate_part = jnp.dot(slab, gate_weight[index], preferred_element_type=jnp.float32)
    up_part = jnp.dot(slab, up_weight[index], preferred_element_type=jnp.float32)
    activation = (jax.nn.silu(gate_part) * up_part).astype(jnp.bfloat16)
    return jnp.dot(activation, down_weight[index], preferred_element_type=jnp.float32).astype(jnp.bfloat16)

def reference(queries, keys, values, out_weight, residual_in, gate_weight, up_weight, down_weight, expert_ids, route_gates):
    scale = HEAD_DIM ** (-0.5)
    head_count = queries.shape[1] // HEAD_DIM

    def head_output(head):
        offset = (head * HEAD_DIM).astype(jnp.int32)
        query_h = lax.dynamic_slice_in_dim(queries, offset, HEAD_DIM, 1)
        key_h = lax.dynamic_slice_in_dim(keys, offset, HEAD_DIM, 1)
        value_h = lax.dynamic_slice_in_dim(values, offset, HEAD_DIM, 1)
        scores = jnp.dot(query_h, key_h.T, preferred_element_type=jnp.float32) * scale
        weights = jnp.exp(scores - lax.optimization_barrier(jnp.max(scores, axis=1, keepdims=True)))
        numerator = jnp.dot(weights.astype(jnp.bfloat16), value_h, preferred_element_type=jnp.float32)
        return (numerator / lax.optimization_barrier(jnp.sum(weights, axis=1, keepdims=True))).astype(jnp.bfloat16)
    per_head = lax.map(head_output, jnp.arange(head_count, dtype=jnp.int32))
    attention = jnp.transpose(per_head, (1, 0, 2)).reshape(queries.shape[0], head_count * HEAD_DIM)
    hidden = residual_in.astype(jnp.float32) + jnp.dot(attention, out_weight, preferred_element_type=jnp.float32)
    normed = (hidden * lax.rsqrt(lax.optimization_barrier(jnp.mean(hidden * hidden, axis=1, keepdims=True)) + 1e-06)).astype(jnp.bfloat16)
    flat_ids = expert_ids.reshape(-1)
    order = jnp.argsort(flat_ids, stable=True).astype(jnp.int32)
    sorted_ids = flat_ids[order]
    sorted_rows = normed[order // 2]
    tile_size = 64
    id_tiles = sorted_ids.reshape(-1, tile_size)
    row_tiles = sorted_rows.reshape(-1, tile_size, D)

    def one_tile(packed):
        tile_ids, tile_rows = packed

        def add_expert(index, totals):
            result = expert_apply(index, tile_rows, gate_weight, up_weight, down_weight)
            return totals + jnp.where((tile_ids == index)[:, None], result.astype(jnp.float32), jnp.float32(0.0))
        return lax.fori_loop(tile_ids[0], tile_ids[-1] + 1, add_expert, jnp.zeros((tile_size, D), jnp.float32))
    outputs = lax.map(one_tile, (id_tiles, row_tiles)).reshape(-1, D)
    per_route = jnp.zeros_like(outputs).at[order].set(outputs).reshape(-1, 2, D)
    combined = per_route[:, 0, :] * route_gates[:, 0:1] + per_route[:, 1, :] * route_gates[:, 1:2]
    return (hidden + combined).astype(jnp.bfloat16)
```

```python
import jax
import jax.numpy as jnp
from jax import lax
from jax.sharding import PartitionSpec as P

D = 2048
HEAD_DIM = 128
CAP = 16


def per_device(
    queries,
    keys,
    values,
    out_weight,
    residual_in,
    gate_weight,
    up_weight,
    down_weight,
    expert_ids,
    route_gates,
):
    scale = HEAD_DIM ** (-0.5)
    local_tokens = queries.shape[0]
    head_count = queries.shape[1] // HEAD_DIM
    query_heads = queries.reshape(local_tokens, head_count, HEAD_DIM)
    key_piece = lax.all_gather(keys, "ctx", axis=0, tiled=True)
    value_piece = lax.all_gather(values, "ctx", axis=0, tiled=True)
    count = key_piece.shape[0]
    key_heads = key_piece.reshape(count, head_count, HEAD_DIM)
    value_heads = value_piece.reshape(count, head_count, HEAD_DIM)
    running_max = jnp.full((head_count, local_tokens), -1e30, jnp.float32)
    scores = (
        jnp.einsum("qhd,khd->hqk", query_heads, key_heads, preferred_element_type=jnp.float32)
        * scale
    )
    newest_max = jnp.maximum(running_max, jnp.max(scores, axis=2))
    weights = jnp.exp(scores - newest_max[:, :, None])
    numerator = jnp.einsum(
        "hqk,khd->hqd",
        weights.astype(jnp.bfloat16),
        value_heads,
        preferred_element_type=jnp.float32,
    )
    denominator = jnp.sum(weights, axis=2)
    final_max, numerator, denominator = (newest_max, numerator, denominator)
    attention = (numerator / denominator[:, :, None]).astype(jnp.bfloat16)
    attention = jnp.transpose(attention, (1, 0, 2)).reshape(local_tokens, head_count * HEAD_DIM)
    own_rows = residual_in.shape[0]
    hidden = residual_in.astype(jnp.float32) + lax.psum_scatter(
        jnp.dot(attention, out_weight, preferred_element_type=jnp.float32).astype(jnp.bfloat16),
        "exp",
        scatter_dimension=0,
        tiled=True,
    ).astype(jnp.float32)
    normed = (hidden * lax.rsqrt(jnp.mean(hidden * hidden, axis=1, keepdims=True) + 1e-06)).astype(
        jnp.bfloat16
    )
    owners = lax.axis_size("exp")
    flat_ids = expert_ids.reshape(-1)
    one_hot = (flat_ids[:, None] == jnp.arange(owners, dtype=jnp.int32)[None, :]).astype(jnp.int32)
    earlier = jnp.cumsum(one_hot, axis=0) - one_hot
    slot_index = jnp.sum(earlier * one_hot, axis=1)
    target = flat_ids * CAP + slot_index
    dispatch_table = (target[None, :] == jnp.arange(owners * CAP, dtype=jnp.int32)[:, None]).astype(
        jnp.bfloat16
    )
    routed = jnp.repeat(normed, 2, axis=0)
    outgoing = jnp.dot(dispatch_table, routed, preferred_element_type=jnp.float32).astype(
        jnp.bfloat16
    )
    incoming = lax.all_to_all(
        outgoing.reshape(owners, CAP, D), "exp", split_axis=0, concat_axis=0, tiled=True
    )
    slot_rows = incoming.reshape(owners * CAP, D)
    gate_part = jnp.dot(
        slot_rows,
        lax.all_gather(gate_weight[0], "ctx", axis=0, tiled=True),
        preferred_element_type=jnp.float32,
    )
    up_part = jnp.dot(
        slot_rows,
        lax.all_gather(up_weight[0], "ctx", axis=0, tiled=True),
        preferred_element_type=jnp.float32,
    )
    activation = (jax.nn.silu(gate_part) * up_part).astype(jnp.bfloat16)
    expert_result = jnp.dot(
        activation,
        lax.all_gather(down_weight[0], "ctx", axis=1, tiled=True),
        preferred_element_type=jnp.float32,
    ).astype(jnp.bfloat16)
    returned = lax.all_to_all(
        expert_result.reshape(owners, CAP, D), "exp", split_axis=0, concat_axis=0, tiled=True
    )
    per_route = jnp.einsum(
        "sr,sd->rd",
        dispatch_table,
        returned.reshape(owners * CAP, D),
        preferred_element_type=jnp.float32,
    )
    per_route = per_route.reshape(own_rows, 2, D)
    combined = per_route[:, 0, :] * route_gates[:, 0:1] + per_route[:, 1, :] * route_gates[:, 1:2]
    return (hidden + combined).astype(jnp.bfloat16)


def per_device_pair(
    queries,
    keys,
    values,
    out_weight,
    residual_in,
    gate_weight,
    up_weight,
    down_weight,
    expert_ids,
    route_gates,
):
    scale = HEAD_DIM ** (-0.5)
    local_tokens = queries.shape[0]
    head_count = queries.shape[1] // HEAD_DIM
    swap = [(0, 1), (1, 0)]
    me = lax.axis_index("ctx")
    key_other = lax.ppermute(keys, "ctx", swap)
    value_other = lax.ppermute(values, "ctx", swap)
    query_heads = queries.reshape(local_tokens, head_count, HEAD_DIM)
    key_heads = jnp.concatenate([keys, key_other], 0).reshape(-1, head_count, HEAD_DIM)
    value_heads = jnp.concatenate([values, value_other], 0).reshape(-1, head_count, HEAD_DIM)
    scores = (
        jnp.einsum("qhd,khd->hqk", query_heads, key_heads, preferred_element_type=jnp.float32)
        * scale
    )
    weights = jnp.exp(scores - jnp.max(scores, axis=2, keepdims=True))
    numerator = jnp.einsum(
        "hqk,khd->hqd",
        weights.astype(jnp.bfloat16),
        value_heads,
        preferred_element_type=jnp.float32,
    )
    attention = (numerator / jnp.sum(weights, axis=2, keepdims=True)).astype(jnp.bfloat16)
    attention = jnp.transpose(attention, (1, 0, 2)).reshape(local_tokens, head_count * HEAD_DIM)
    own_rows = residual_in.shape[0]
    hidden = residual_in.astype(jnp.float32) + lax.psum_scatter(
        jnp.dot(attention, out_weight, preferred_element_type=jnp.float32).astype(jnp.bfloat16),
        "exp",
        scatter_dimension=0,
        tiled=True,
    ).astype(jnp.float32)
    normed = (hidden * lax.rsqrt(jnp.mean(hidden * hidden, axis=1, keepdims=True) + 1e-06)).astype(
        jnp.bfloat16
    )
    owners = lax.axis_size("exp")
    slots = owners * CAP
    half = D // 2
    flat_ids = expert_ids.reshape(-1)
    one_hot = (flat_ids[:, None] == jnp.arange(owners, dtype=jnp.int32)[None, :]).astype(jnp.int32)
    earlier = jnp.cumsum(one_hot, axis=0) - one_hot
    target = flat_ids * CAP + jnp.sum(earlier * one_hot, axis=1)
    dispatch_table = (target[None, :] == jnp.arange(slots, dtype=jnp.int32)[:, None]).astype(
        jnp.bfloat16
    )
    routed = jnp.repeat(normed, 2, axis=0)
    halves = [
        jnp.dot(
            dispatch_table, routed[:, c * half : (c + 1) * half], preferred_element_type=jnp.float32
        ).astype(jnp.bfloat16)
        for c in range(2)
    ]
    incoming = lax.all_to_all(
        jnp.concatenate(halves, 0).reshape(2 * owners, CAP, half),
        ("ctx", "exp"),
        split_axis=0,
        concat_axis=0,
        tiled=True,
    )
    slot_rows = incoming.reshape(2 * slots, half)
    part = jnp.concatenate(
        [
            jnp.dot(slot_rows, gate_weight[0], preferred_element_type=jnp.float32),
            jnp.dot(slot_rows, up_weight[0], preferred_element_type=jnp.float32),
        ],
        1,
    )
    mine = lax.dynamic_slice_in_dim(part, me * slots, slots, 0)
    theirs = lax.dynamic_slice_in_dim(part, (1 - me) * slots, slots, 0)
    whole = mine + lax.ppermute(theirs.astype(jnp.bfloat16), "ctx", swap).astype(jnp.float32)
    hidden_units = gate_weight.shape[2]
    activation = (jax.nn.silu(whole[:, :hidden_units]) * whole[:, hidden_units:]).astype(
        jnp.bfloat16
    )
    other = lax.ppermute(activation, "ctx", swap)
    first = jnp.where(me == 0, activation, other)
    second = jnp.where(me == 0, other, activation)
    expert_result = jnp.dot(
        jnp.concatenate([first, second], 0), down_weight[0], preferred_element_type=jnp.float32
    ).astype(jnp.bfloat16)
    returned = lax.all_to_all(
        expert_result.reshape(2 * owners, CAP, half),
        ("ctx", "exp"),
        split_axis=0,
        concat_axis=0,
        tiled=True,
    ).reshape(2, slots, half)
    per_route = jnp.concatenate(
        [
            jnp.einsum(
                "sr,sd->rd", dispatch_table, returned[c], preferred_element_type=jnp.float32
            )
            for c in range(2)
        ],
        1,
    ).reshape(own_rows, 2, D)
    combined = per_route[:, 0, :] * route_gates[:, 0:1] + per_route[:, 1, :] * route_gates[:, 1:2]
    return (hidden + combined).astype(jnp.bfloat16)


def solution(mesh):
    return jax.shard_map(
        per_device_pair if mesh.shape["ctx"] == 2 else per_device,
        mesh=mesh,
        in_specs=(
            P(("group", "ctx"), "exp"),
            P(("group", "ctx"), "exp"),
            P(("group", "ctx"), "exp"),
            P("exp", None),
            P(("group", "ctx", "exp"), None),
            P("exp", "ctx", None),
            P("exp", "ctx", None),
            P("exp", None, "ctx"),
            P(("group", "ctx", "exp"), None),
            P(("group", "ctx", "exp"), None),
        ),
        out_specs=P(("group", "ctx", "exp"), None),
        check_vma=False,
    )
```

```python
import functools

import jax
import jax.numpy as jnp
from jax import lax
from jax.experimental import pallas as pl
from jax.experimental.pallas import tpu as pltpu
from jax.sharding import PartitionSpec as P

D = 2048
HEAD_DIM = 128
CAP = 16


def per_device(
    queries,
    keys,
    values,
    out_weight,
    residual_in,
    gate_weight,
    up_weight,
    down_weight,
    expert_ids,
    route_gates,
):
    scale = HEAD_DIM ** (-0.5)
    local_tokens = queries.shape[0]
    head_count = queries.shape[1] // HEAD_DIM
    query_heads = queries.reshape(local_tokens, head_count, HEAD_DIM)
    key_piece = lax.all_gather(keys, "ctx", axis=0, tiled=True)
    value_piece = lax.all_gather(values, "ctx", axis=0, tiled=True)
    count = key_piece.shape[0]
    key_heads = key_piece.reshape(count, head_count, HEAD_DIM)
    value_heads = value_piece.reshape(count, head_count, HEAD_DIM)
    running_max = jnp.full((head_count, local_tokens), -1e30, jnp.float32)
    scores = (
        jnp.einsum("qhd,khd->hqk", query_heads, key_heads, preferred_element_type=jnp.float32)
        * scale
    )
    newest_max = jnp.maximum(running_max, jnp.max(scores, axis=2))
    weights = jnp.exp(scores - newest_max[:, :, None])
    numerator = jnp.einsum(
        "hqk,khd->hqd",
        weights.astype(jnp.bfloat16),
        value_heads,
        preferred_element_type=jnp.float32,
    )
    denominator = jnp.sum(weights, axis=2)
    final_max, numerator, denominator = (newest_max, numerator, denominator)
    attention = (numerator / denominator[:, :, None]).astype(jnp.bfloat16)
    attention = jnp.transpose(attention, (1, 0, 2)).reshape(local_tokens, head_count * HEAD_DIM)
    own_rows = residual_in.shape[0]
    hidden = residual_in.astype(jnp.float32) + lax.psum_scatter(
        jnp.dot(attention, out_weight, preferred_element_type=jnp.float32).astype(jnp.bfloat16),
        "exp",
        scatter_dimension=0,
        tiled=True,
    ).astype(jnp.float32)
    normed = (hidden * lax.rsqrt(jnp.mean(hidden * hidden, axis=1, keepdims=True) + 1e-06)).astype(
        jnp.bfloat16
    )
    owners = lax.axis_size("exp")
    flat_ids = expert_ids.reshape(-1)
    one_hot = (flat_ids[:, None] == jnp.arange(owners, dtype=jnp.int32)[None, :]).astype(jnp.int32)
    earlier = jnp.cumsum(one_hot, axis=0) - one_hot
    slot_index = jnp.sum(earlier * one_hot, axis=1)
    target = flat_ids * CAP + slot_index
    dispatch_table = (target[None, :] == jnp.arange(owners * CAP, dtype=jnp.int32)[:, None]).astype(
        jnp.bfloat16
    )
    routed = jnp.repeat(normed, 2, axis=0)
    outgoing = jnp.dot(dispatch_table, routed, preferred_element_type=jnp.float32).astype(
        jnp.bfloat16
    )
    incoming = lax.all_to_all(
        outgoing.reshape(owners, CAP, D), "exp", split_axis=0, concat_axis=0, tiled=True
    )
    slot_rows = incoming.reshape(owners * CAP, D)
    gate_part = jnp.dot(
        slot_rows,
        lax.all_gather(gate_weight[0], "ctx", axis=0, tiled=True),
        preferred_element_type=jnp.float32,
    )
    up_part = jnp.dot(
        slot_rows,
        lax.all_gather(up_weight[0], "ctx", axis=0, tiled=True),
        preferred_element_type=jnp.float32,
    )
    activation = (jax.nn.silu(gate_part) * up_part).astype(jnp.bfloat16)
    expert_result = jnp.dot(
        activation,
        lax.all_gather(down_weight[0], "ctx", axis=1, tiled=True),
        preferred_element_type=jnp.float32,
    ).astype(jnp.bfloat16)
    returned = lax.all_to_all(
        expert_result.reshape(owners, CAP, D), "exp", split_axis=0, concat_axis=0, tiled=True
    )
    per_route = jnp.einsum(
        "sr,sd->rd",
        dispatch_table,
        returned.reshape(owners * CAP, D),
        preferred_element_type=jnp.float32,
    )
    per_route = per_route.reshape(own_rows, 2, D)
    combined = per_route[:, 0, :] * route_gates[:, 0:1] + per_route[:, 1, :] * route_gates[:, 1:2]
    return (hidden + combined).astype(jnp.bfloat16)


F32 = jnp.float32
BF16 = jnp.bfloat16
HALF = D // 2


def dot(a, b):
    return jnp.dot(a, b, preferred_element_type=F32)


def block_kernel(
    owners,
    q_ref,
    k_ref,
    v_ref,
    wo_hbm,
    res_ref,
    wg_hbm,
    wu_hbm,
    wd_hbm,
    ids_ref,
    gates_ref,
    out_ref,
    wo,
    wg,
    wu,
    wd,
    k_other,
    v_other,
    q_sorted,
    attn,
    mate_out,
    mate_in,
    own_part,
    reduce_out,
    reduce_in,
    hidden,
    outgoing,
    slab,
    part_out,
    part_in,
    act_own,
    act_other,
    results,
    returned,
    load_sem,
    kv_send,
    kv_recv,
    mate_send,
    mate_recv,
    red_send,
    red_recv,
    disp_send,
    disp_recv,
    part_send,
    part_recv,
    act_send,
    act_recv,
    ret_send,
    ret_recv,
):
    chips = owners // 2
    ctx = lax.axis_index("ctx")
    exp = lax.axis_index("exp")
    chip, core = exp // 2, lax.rem(exp, 2)
    rows = res_ref.shape[0]
    slots = owners * CAP
    group_rows = chips * rows
    other_ctx = 1 - ctx

    def place(dc, de):
        return {
            "ctx": other_ctx if dc else ctx,
            "exp": lax.rem(exp + de, owners) if de else exp,
        }

    def remote(src, dst, send, recv, where):
        copy = pltpu.make_async_remote_copy(
            src_ref=src,
            dst_ref=dst,
            send_sem=send,
            recv_sem=recv,
            device_id=where,
            device_id_type=pl.DeviceIdType.MESH,
        )
        copy.start()
        return copy

    loads = []
    for n, (src, dst) in enumerate(((wo_hbm, wo), (wg_hbm, wg), (wu_hbm, wu), (wd_hbm, wd))):
        load = pltpu.make_async_copy(src, dst, load_sem.at[n])
        load.start()
        loads.append(load)

    partners = [(dc, de) for dc in range(2) for de in range(owners) if dc or de]
    barrier = pltpu.get_barrier_semaphore()
    for dc, de in partners:
        pl.semaphore_signal(
            barrier, inc=1, device_id=place(dc, de), device_id_type=pl.DeviceIdType.MESH
        )
    pl.semaphore_wait(barrier, len(partners))

    across = place(1, 0)
    k_copy = remote(k_ref, k_other, kv_send.at[0], kv_recv.at[0], across)
    v_copy = remote(v_ref, v_other, kv_send.at[1], kv_recv.at[1], across)

    lane = lax.broadcasted_iota(jnp.int32, (rows, slots), 1)
    picks = []
    for k in range(2):
        rel = ids_ref[:, k : k + 1] - exp
        picks.append(jnp.where(rel < 0, rel + owners, rel))
    named = [jnp.where(lane == rel, 1.0, 0.0) for rel in picks]
    below = jnp.where(
        lax.broadcasted_iota(jnp.int32, (rows, rows), 0)
        > lax.broadcasted_iota(jnp.int32, (rows, rows), 1),
        1.0,
        0.0,
    )
    earlier = dot(below.astype(BF16), (named[0] + named[1]).astype(BF16))
    tables = []
    for k in range(2):
        slot = jnp.sum(earlier * named[k], axis=1, keepdims=True)
        target = picks[k].astype(F32) * CAP + slot
        tables.append(jnp.where(lane.astype(F32) == target, 1.0, 0.0))
    dispatch_t = (tables[0] + tables[1]).T.astype(BF16)
    combine = jnp.concatenate(tables, 0).astype(BF16)

    for half in range(2):
        keeper = core if half else 1 - core
        for z in range(chips):
            start = pl.multiple_of((2 * z + keeper) * rows, rows)
            q_sorted[pl.ds((half * chips + z) * rows, rows), :] = q_ref[pl.ds(start, rows), :]

    scale = HEAD_DIM ** (-0.5)
    head_count = q_ref.shape[1] // HEAD_DIM
    contract = (((1,), (1,)), ((), ()))

    def scores_of(half, h, keys):
        cols = pl.ds(h * HEAD_DIM, HEAD_DIM)
        return (
            lax.dot_general(
                q_sorted[pl.ds(half * group_rows, group_rows), cols],
                keys[:, cols],
                contract,
                preferred_element_type=F32,
            )
            * scale
        )

    def attend(half):
        for h in range(head_count):
            cols = pl.ds(h * HEAD_DIM, HEAD_DIM)
            near, far = scores_of(half, h, k_ref), scores_of(half, h, k_other)
            top = jnp.maximum(
                jnp.max(near, axis=1, keepdims=True), jnp.max(far, axis=1, keepdims=True)
            )
            near, far = jnp.exp(near - top), jnp.exp(far - top)
            total = jnp.sum(near, axis=1, keepdims=True) + jnp.sum(far, axis=1, keepdims=True)
            numerator = dot(near.astype(BF16), v_ref[:, cols]) + dot(
                far.astype(BF16), v_other[:, cols]
            )
            attn[:, cols] = (numerator / total).astype(BF16)

    k_copy.wait_recv()
    v_copy.wait_recv()
    mate = {"ctx": ctx, "exp": exp + 1 - 2 * core}
    attend(0)
    loads[0].wait()
    mate_out[...] = dot(attn[...], wo[...]).astype(BF16)
    mate_copy = remote(mate_out, mate_in, mate_send, mate_recv, mate)
    attend(1)
    own_part[...] = dot(attn[...], wo[...])
    mate_copy.wait_recv()
    red_copies = []
    for dz in range(chips - 1, 0, -1):
        to_chip = lax.rem(chip + dz, chips)
        start = pl.multiple_of(to_chip * rows, rows)
        reduce_out[dz - 1] = (
            own_part[pl.ds(start, rows), :] + mate_in[pl.ds(start, rows), :].astype(F32)
        ).astype(BF16)
        red_copies.append(
            remote(
                reduce_out.at[dz - 1],
                reduce_in.at[dz - 1],
                red_send.at[dz - 1],
                red_recv.at[dz - 1],
                {"ctx": ctx, "exp": 2 * to_chip + core},
            )
        )
    start = pl.multiple_of(chip * rows, rows)
    hidden[...] = (
        res_ref[...].astype(F32)
        + own_part[pl.ds(start, rows), :]
        + mate_in[pl.ds(start, rows), :].astype(F32)
    )
    for dz, copy in zip(range(chips - 1, 0, -1), red_copies):
        copy.wait_recv()
        hidden[...] += reduce_in[dz - 1].astype(F32)

    square = jnp.mean(hidden[...] * hidden[...], axis=1, keepdims=True)
    normed = (hidden[...] * lax.rsqrt(square + 1e-06)).astype(BF16)
    for c in range(2):
        sent = dot(dispatch_t, normed[:, c * HALF : (c + 1) * HALF]).astype(BF16)
        outgoing[c] = sent.reshape(owners, CAP, HALF)
    disp_copies = {}
    order = sorted(partners, key=lambda p: (-p[0], abs(p[1] - owners // 2)))
    for dc, de in order:
        disp_copies[dc, de] = remote(
            outgoing.at[other_ctx if dc else ctx, de],
            slab.at[dc, de],
            disp_send.at[dc, de],
            disp_recv.at[dc, de],
            place(dc, de),
        )
    slab[0, 0] = outgoing[ctx, 0]
    for de in range(owners):
        disp_copies[1, de].wait_recv()
    loads[1].wait()
    loads[2].wait()
    far_rows = slab[1].reshape(slots, HALF)
    part_copies = []
    for n, weight in enumerate((wg, wu)):
        part_out[n] = dot(far_rows, weight[...]).astype(BF16)
        part_copies.append(
            remote(part_out.at[n], part_in.at[n], part_send.at[n], part_recv.at[n], across)
        )
    for de in range(1, owners):
        disp_copies[0, de].wait_recv()
    near_rows = slab[0].reshape(slots, HALF)
    gate_part = dot(near_rows, wg[...])
    up_part = dot(near_rows, wu[...])
    part_copies[0].wait_recv()
    gate_part = gate_part + part_in[0].astype(F32)
    gate_part = gate_part / (1.0 + jnp.exp(-gate_part))
    part_copies[1].wait_recv()
    act_own[...] = (gate_part * (up_part + part_in[1].astype(F32))).astype(BF16)
    act_copy = remote(act_own, act_other, act_send, act_recv, across)
    loads[3].wait()
    ret_copies = {}
    for dc in range(2):
        if dc:
            act_copy.wait_recv()
        result = dot((act_other if dc else act_own)[...], wd[...]).astype(BF16)
        results[dc] = result.reshape(owners, CAP, HALF)
        for de in sorted(range(owners), key=lambda e: abs(e - owners // 2)):
            if dc or de:
                ret_copies[dc, de] = remote(
                    results.at[dc, de],
                    returned.at[dc, de],
                    ret_send.at[dc, de],
                    ret_recv.at[dc, de],
                    place(dc, owners - de if de else 0),
                )
    returned[0, 0] = results[0, 0]
    for dc in range(2):
        for de in range(owners):
            if dc or de:
                ret_copies[dc, de].wait_recv()
        per_route = dot(combine, returned[dc].reshape(slots, HALF))
        cols = pl.ds(pl.multiple_of((other_ctx if dc else ctx) * HALF, HALF), HALF)
        out_ref[:, cols] = (
            hidden[:, cols]
            + per_route[:rows] * gates_ref[:, 0:1]
            + per_route[rows:] * gates_ref[:, 1:2]
        ).astype(BF16)

    for copy in (
        [k_copy, v_copy, mate_copy, act_copy]
        + red_copies
        + part_copies
        + list(disp_copies.values())
        + list(ret_copies.values())
    ):
        copy.wait_send()


def per_device_pair(
    owners,
    queries,
    keys,
    values,
    out_weight,
    residual_in,
    gate_weight,
    up_weight,
    down_weight,
    expert_ids,
    route_gates,
):
    tokens, width = queries.shape
    rows = residual_in.shape[0]
    units = gate_weight.shape[2]
    chips, slots = owners // 2, owners * CAP
    in_vmem = pl.BlockSpec(memory_space=pltpu.VMEM)
    anywhere = pl.BlockSpec(memory_space=pl.ANY)
    dma = pltpu.SemaphoreType.DMA
    return pl.pallas_call(
        functools.partial(block_kernel, owners),
        out_shape=jax.ShapeDtypeStruct((rows, D), BF16),
        in_specs=[in_vmem] * 3
        + [anywhere, in_vmem, anywhere, anywhere, anywhere, in_vmem, in_vmem],
        out_specs=in_vmem,
        scratch_shapes=[
            pltpu.VMEM((width, D), BF16),
            pltpu.VMEM((HALF, units), BF16),
            pltpu.VMEM((HALF, units), BF16),
            pltpu.VMEM((units, HALF), BF16),
            pltpu.VMEM((tokens, width), BF16),
            pltpu.VMEM((tokens, width), BF16),
            pltpu.VMEM((tokens, width), BF16),
            pltpu.VMEM((chips * rows, width), BF16),
            pltpu.VMEM((chips * rows, D), BF16),
            pltpu.VMEM((chips * rows, D), BF16),
            pltpu.VMEM((chips * rows, D), F32),
            pltpu.VMEM((chips - 1, rows, D), BF16),
            pltpu.VMEM((chips - 1, rows, D), BF16),
            pltpu.VMEM((rows, D), F32),
            pltpu.VMEM((2, owners, CAP, HALF), BF16),
            pltpu.VMEM((2, owners, CAP, HALF), BF16),
            pltpu.VMEM((2, slots, units), BF16),
            pltpu.VMEM((2, slots, units), BF16),
            pltpu.VMEM((slots, units), BF16),
            pltpu.VMEM((slots, units), BF16),
            pltpu.VMEM((2, owners, CAP, HALF), BF16),
            pltpu.VMEM((2, owners, CAP, HALF), BF16),
            dma((4,)),
            dma((2,)),
            dma((2,)),
            dma,
            dma,
            dma((chips - 1,)),
            dma((chips - 1,)),
            dma((2, owners)),
            dma((2, owners)),
            dma((2,)),
            dma((2,)),
            dma,
            dma,
            dma((2, owners)),
            dma((2, owners)),
        ],
        compiler_params=pltpu.CompilerParams(
            collective_id=0, has_side_effects=True, vmem_limit_bytes=40 * 1024 * 1024
        ),
    )(
        queries,
        keys,
        values,
        out_weight,
        residual_in,
        gate_weight[0],
        up_weight[0],
        down_weight[0],
        expert_ids,
        route_gates,
    )


def solution(mesh):
    if mesh.shape["ctx"] == 2 and mesh.shape["exp"] % 2 == 0:
        body = functools.partial(per_device_pair, mesh.shape["exp"])
    else:
        body = per_device
    return jax.shard_map(
        body,
        mesh=mesh,
        in_specs=(
            P(("group", "ctx"), "exp"),
            P(("group", "ctx"), "exp"),
            P(("group", "ctx"), "exp"),
            P("exp", None),
            P(("group", "ctx", "exp"), None),
            P("exp", "ctx", None),
            P("exp", "ctx", None),
            P("exp", None, "ctx"),
            P(("group", "ctx", "exp"), None),
            P(("group", "ctx", "exp"), None),
        ),
        out_specs=P(("group", "ctx", "exp"), None),
        check_vma=False,
    )
```

```python
import functools

import jax
import jax.numpy as jnp
from jax import lax
from jax.experimental import pallas as pl
from jax.experimental.pallas import tpu as pltpu
from jax.sharding import PartitionSpec as P

D = 2048
HEAD_DIM = 128
CAP = 16


def per_device(
    queries,
    keys,
    values,
    out_weight,
    residual_in,
    gate_weight,
    up_weight,
    down_weight,
    expert_ids,
    route_gates,
):
    scale = HEAD_DIM ** (-0.5)
    local_tokens = queries.shape[0]
    head_count = queries.shape[1] // HEAD_DIM
    query_heads = queries.reshape(local_tokens, head_count, HEAD_DIM)
    key_piece = lax.all_gather(keys, "ctx", axis=0, tiled=True)
    value_piece = lax.all_gather(values, "ctx", axis=0, tiled=True)
    count = key_piece.shape[0]
    key_heads = key_piece.reshape(count, head_count, HEAD_DIM)
    value_heads = value_piece.reshape(count, head_count, HEAD_DIM)
    running_max = jnp.full((head_count, local_tokens), -1e30, jnp.float32)
    scores = (
        jnp.einsum("qhd,khd->hqk", query_heads, key_heads, preferred_element_type=jnp.float32)
        * scale
    )
    newest_max = jnp.maximum(running_max, jnp.max(scores, axis=2))
    weights = jnp.exp(scores - newest_max[:, :, None])
    numerator = jnp.einsum(
        "hqk,khd->hqd",
        weights.astype(jnp.bfloat16),
        value_heads,
        preferred_element_type=jnp.float32,
    )
    denominator = jnp.sum(weights, axis=2)
    final_max, numerator, denominator = (newest_max, numerator, denominator)
    attention = (numerator / denominator[:, :, None]).astype(jnp.bfloat16)
    attention = jnp.transpose(attention, (1, 0, 2)).reshape(local_tokens, head_count * HEAD_DIM)
    own_rows = residual_in.shape[0]
    hidden = residual_in.astype(jnp.float32) + lax.psum_scatter(
        jnp.dot(attention, out_weight, preferred_element_type=jnp.float32).astype(jnp.bfloat16),
        "exp",
        scatter_dimension=0,
        tiled=True,
    ).astype(jnp.float32)
    normed = (hidden * lax.rsqrt(jnp.mean(hidden * hidden, axis=1, keepdims=True) + 1e-06)).astype(
        jnp.bfloat16
    )
    owners = lax.axis_size("exp")
    flat_ids = expert_ids.reshape(-1)
    one_hot = (flat_ids[:, None] == jnp.arange(owners, dtype=jnp.int32)[None, :]).astype(jnp.int32)
    earlier = jnp.cumsum(one_hot, axis=0) - one_hot
    slot_index = jnp.sum(earlier * one_hot, axis=1)
    target = flat_ids * CAP + slot_index
    dispatch_table = (target[None, :] == jnp.arange(owners * CAP, dtype=jnp.int32)[:, None]).astype(
        jnp.bfloat16
    )
    routed = jnp.repeat(normed, 2, axis=0)
    outgoing = jnp.dot(dispatch_table, routed, preferred_element_type=jnp.float32).astype(
        jnp.bfloat16
    )
    incoming = lax.all_to_all(
        outgoing.reshape(owners, CAP, D), "exp", split_axis=0, concat_axis=0, tiled=True
    )
    slot_rows = incoming.reshape(owners * CAP, D)
    gate_part = jnp.dot(
        slot_rows,
        lax.all_gather(gate_weight[0], "ctx", axis=0, tiled=True),
        preferred_element_type=jnp.float32,
    )
    up_part = jnp.dot(
        slot_rows,
        lax.all_gather(up_weight[0], "ctx", axis=0, tiled=True),
        preferred_element_type=jnp.float32,
    )
    activation = (jax.nn.silu(gate_part) * up_part).astype(jnp.bfloat16)
    expert_result = jnp.dot(
        activation,
        lax.all_gather(down_weight[0], "ctx", axis=1, tiled=True),
        preferred_element_type=jnp.float32,
    ).astype(jnp.bfloat16)
    returned = lax.all_to_all(
        expert_result.reshape(owners, CAP, D), "exp", split_axis=0, concat_axis=0, tiled=True
    )
    per_route = jnp.einsum(
        "sr,sd->rd",
        dispatch_table,
        returned.reshape(owners * CAP, D),
        preferred_element_type=jnp.float32,
    )
    per_route = per_route.reshape(own_rows, 2, D)
    combined = per_route[:, 0, :] * route_gates[:, 0:1] + per_route[:, 1, :] * route_gates[:, 1:2]
    return (hidden + combined).astype(jnp.bfloat16)


F32 = jnp.float32
BF16 = jnp.bfloat16
HALF = D // 2


def dot(a, b):
    return jnp.dot(a, b, preferred_element_type=F32)


def block_kernel(
    owners,
    q_hbm,
    k_hbm,
    v_hbm,
    wo_hbm,
    res_hbm,
    wg_hbm,
    wu_hbm,
    wd_hbm,
    ids_hbm,
    gates_hbm,
    out_ref,
    k_ref,
    v_ref,
    res_ref,
    ids_ref,
    gates_ref,
    wo,
    wg,
    wu,
    wd,
    k_other,
    v_other,
    q_sorted,
    attn,
    mate_out,
    mate_in,
    own_part,
    reduce_out,
    reduce_in,
    hidden,
    outgoing,
    slab,
    part_out,
    part_in,
    act_own,
    act_other,
    results,
    returned,
    load_sem,
    q_sem,
    kv_send,
    kv_recv,
    mate_send,
    mate_recv,
    red_send,
    red_recv,
    disp_send,
    disp_recv,
    part_send,
    part_recv,
    act_send,
    act_recv,
    ret_send,
    ret_recv,
):
    chips = owners // 2
    ctx = lax.axis_index("ctx")
    exp = lax.axis_index("exp")
    chip, core = exp // 2, lax.rem(exp, 2)
    rows = res_ref.shape[0]
    slots = owners * CAP
    group_rows = chips * rows
    other_ctx = 1 - ctx

    def place(dc, de):
        return {
            "ctx": other_ctx if dc else ctx,
            "exp": lax.rem(exp + de, owners) if de else exp,
        }

    def dot_t(a, b):
        return lax.dot_general(a, b, (((1,), (1,)), ((), ())), preferred_element_type=F32)

    def remote(src, dst, send, recv, where):
        copy = pltpu.make_async_remote_copy(
            src_ref=src,
            dst_ref=dst,
            send_sem=send,
            recv_sem=recv,
            device_id=where,
            device_id_type=pl.DeviceIdType.MESH,
        )
        copy.start()
        return copy

    def load(n, src, dst):
        copy = pltpu.make_async_copy(src, dst, load_sem.at[n])
        copy.start()
        return copy

    q_loads = []
    for n in range(owners):
        keeper = core if n >= chips else 1 - core
        start = pl.multiple_of((2 * (n % chips) + keeper) * rows, rows)
        copy = pltpu.make_async_copy(
            q_hbm.at[pl.ds(start, rows), :], q_sorted.at[pl.ds(n * rows, rows), :], q_sem.at[n]
        )
        copy.start()
        q_loads.append(copy)
    k_load = load(0, k_hbm, k_ref)
    v_load = load(1, v_hbm, v_ref)
    ids_load = load(2, ids_hbm, ids_ref)
    gates_load = load(3, gates_hbm, gates_ref)
    wo_load = load(4, wo_hbm, wo)
    res_load = load(5, res_hbm, res_ref)
    wg_load = load(6, wg_hbm, wg)
    wu_load = load(7, wu_hbm, wu)
    wd_load = load(8, wd_hbm, wd)

    partners = [(dc, de) for dc in range(2) for de in range(owners) if dc or de]
    barrier = pltpu.get_barrier_semaphore()
    for dc, de in partners:
        pl.semaphore_signal(
            barrier, inc=1, device_id=place(dc, de), device_id_type=pl.DeviceIdType.MESH
        )
    pl.semaphore_wait(barrier, len(partners))

    across = place(1, 0)
    k_copy = remote(k_hbm, k_other, kv_send.at[0], kv_recv.at[0], across)
    v_copy = remote(v_hbm, v_other, kv_send.at[1], kv_recv.at[1], across)

    ids_load.wait()
    gates_load.wait()
    line = lax.broadcasted_iota(jnp.int32, (slots, rows), 0)
    picks = []
    for k in range(2):
        rel = ids_ref[k : k + 1, :] - exp
        picks.append(jnp.where(rel < 0, rel + owners, rel))
    named = [jnp.where(line == rel, 1.0, 0.0) for rel in picks]
    down_row = lax.broadcasted_iota(jnp.int32, (rows, rows), 0)
    down_col = lax.broadcasted_iota(jnp.int32, (rows, rows), 1)
    before = jnp.where(down_row < down_col, 1.0, 0.0)
    same = jnp.where(down_row == down_col, 1.0, 0.0)
    earlier = dot((named[0] + named[1]).astype(BF16), before.astype(BF16))
    tables = []
    for k in range(2):
        slot = jnp.sum(earlier * named[k], axis=0, keepdims=True)
        target = picks[k].astype(F32) * CAP + slot
        tables.append(jnp.where(line.astype(F32) == target, 1.0, 0.0))
    dispatch_t = (tables[0] + tables[1]).astype(BF16)
    combine = jnp.concatenate([table.T for table in tables], 0).astype(BF16)
    gate_columns = [
        jnp.sum(same * gates_ref[k : k + 1, :], axis=1, keepdims=True) for k in range(2)
    ]

    scale = HEAD_DIM ** (-0.5)
    head_count = q_sorted.shape[1] // HEAD_DIM
    contract = (((1,), (1,)), ((), ()))

    def scores_of(half, h, keys):
        cols = pl.ds(h * HEAD_DIM, HEAD_DIM)
        return (
            lax.dot_general(
                q_sorted[pl.ds(half * group_rows, group_rows), cols],
                keys[:, cols],
                contract,
                preferred_element_type=F32,
            )
            * scale
        )

    for copy in q_loads:
        copy.wait()
    k_load.wait()
    v_load.wait()
    near_scores = {}
    for half in range(2):
        for h in range(head_count):
            near_scores[half, h] = scores_of(half, h, k_ref)

    def attend(half):
        for h in range(head_count):
            cols = pl.ds(h * HEAD_DIM, HEAD_DIM)
            near, far = near_scores[half, h], scores_of(half, h, k_other)
            top = jnp.maximum(
                jnp.max(near, axis=1, keepdims=True), jnp.max(far, axis=1, keepdims=True)
            )
            near, far = jnp.exp(near - top), jnp.exp(far - top)
            total = jnp.sum(near, axis=1, keepdims=True) + jnp.sum(far, axis=1, keepdims=True)
            numerator = dot(near.astype(BF16), v_ref[:, cols]) + dot(
                far.astype(BF16), v_other[:, cols]
            )
            attn[:, cols] = (numerator / total).astype(BF16)

    k_copy.wait_recv()
    v_copy.wait_recv()
    mate = {"ctx": ctx, "exp": exp + 1 - 2 * core}
    attend(0)
    wo_load.wait()
    mate_copies = []
    for c in range(2):
        mate_out[c] = dot(attn[...], wo[:, c * HALF : (c + 1) * HALF]).astype(BF16)
        mate_copies.append(
            remote(mate_out.at[c], mate_in.at[c], mate_send.at[c], mate_recv.at[c], mate)
        )
    attend(1)
    red_copies = []
    own_start = pl.multiple_of(chip * rows, rows)
    res_load.wait()
    for c in range(2):
        cols = pl.ds(c * HALF, HALF)
        own_part[...] = dot(attn[...], wo[:, cols])
        mate_copies[c].wait_recv()
        for dz in range(chips - 1, 0, -1):
            to_chip = lax.rem(chip + dz, chips)
            start = pl.multiple_of(to_chip * rows, rows)
            reduce_out[c, dz - 1] = (
                own_part[pl.ds(start, rows), :] + mate_in[c, pl.ds(start, rows), :].astype(F32)
            ).astype(BF16)
            red_copies.append(
                remote(
                    reduce_out.at[c, dz - 1],
                    reduce_in.at[c, dz - 1],
                    red_send.at[c, dz - 1],
                    red_recv.at[c, dz - 1],
                    {"ctx": ctx, "exp": 2 * to_chip + core},
                )
            )
        hidden[:, cols] = (
            res_ref[:, cols].astype(F32)
            + own_part[pl.ds(own_start, rows), :]
            + mate_in[c, pl.ds(own_start, rows), :].astype(F32)
        )
    for c in range(2):
        cols = pl.ds(c * HALF, HALF)
        for dz in range(chips - 1, 0, -1):
            red_copies[c * (chips - 1) + chips - 1 - dz].wait_recv()
            hidden[:, cols] += reduce_in[c, dz - 1].astype(F32)

    square = jnp.mean(hidden[...] * hidden[...], axis=1, keepdims=True)
    normed = (hidden[...] * lax.rsqrt(square + 1e-06)).astype(BF16)
    for c in range(2):
        sent = dot(dispatch_t, normed[:, c * HALF : (c + 1) * HALF]).astype(BF16)
        outgoing[c] = sent.reshape(owners, CAP, HALF)
    disp_copies = {}
    order = sorted(partners, key=lambda p: (-p[0], abs(p[1] - owners // 2)))
    for dc, de in order:
        disp_copies[dc, de] = remote(
            outgoing.at[other_ctx if dc else ctx, de],
            slab.at[dc, de],
            disp_send.at[dc, de],
            disp_recv.at[dc, de],
            place(dc, de),
        )
    slab[0, 0] = outgoing[ctx, 0]
    for de in range(owners):
        disp_copies[1, de].wait_recv()
    wg_load.wait()
    wu_load.wait()
    far_rows = slab[1].reshape(slots, HALF)
    part_copies = []
    for n, weight in enumerate((wg, wu)):
        part_out[n] = dot_t(far_rows, weight[...]).astype(BF16)
        part_copies.append(
            remote(part_out.at[n], part_in.at[n], part_send.at[n], part_recv.at[n], across)
        )
    for de in range(1, owners):
        disp_copies[0, de].wait_recv()
    near_rows = slab[0].reshape(slots, HALF)
    gate_part = dot_t(near_rows, wg[...])
    up_part = dot_t(near_rows, wu[...])
    part_copies[0].wait_recv()
    gate_part = gate_part + part_in[0].astype(F32)
    gate_part = gate_part / (1.0 + jnp.exp(-gate_part))
    part_copies[1].wait_recv()
    act_own[...] = (gate_part * (up_part + part_in[1].astype(F32))).astype(BF16)
    act_copy = remote(act_own, act_other, act_send, act_recv, across)
    wd_load.wait()
    ret_copies = {}
    for dc in range(2):
        if dc:
            act_copy.wait_recv()
        result = dot((act_other if dc else act_own)[...], wd[...]).astype(BF16)
        results[dc] = result.reshape(owners, CAP, HALF)
        for de in sorted(range(owners), key=lambda e: abs(e - owners // 2)):
            if dc or de:
                ret_copies[dc, de] = remote(
                    results.at[dc, de],
                    returned.at[dc, de],
                    ret_send.at[dc, de],
                    ret_recv.at[dc, de],
                    place(dc, owners - de if de else 0),
                )
    returned[0, 0] = results[0, 0]
    for dc in range(2):
        for de in range(owners):
            if dc or de:
                ret_copies[dc, de].wait_recv()
        per_route = dot(combine, returned[dc].reshape(slots, HALF))
        cols = pl.ds(pl.multiple_of((other_ctx if dc else ctx) * HALF, HALF), HALF)
        out_ref[:, cols] = (
            hidden[:, cols]
            + per_route[:rows] * gate_columns[0]
            + per_route[rows:] * gate_columns[1]
        ).astype(BF16)

    for copy in (
        [k_copy, v_copy, act_copy]
        + mate_copies
        + red_copies
        + part_copies
        + list(disp_copies.values())
        + list(ret_copies.values())
    ):
        copy.wait_send()


def per_device_pair(
    owners,
    queries,
    keys,
    values,
    out_weight,
    residual_in,
    gate_weight,
    up_weight,
    down_weight,
    expert_ids,
    route_gates,
):
    tokens, width = queries.shape
    rows = residual_in.shape[0]
    units = gate_weight.shape[2]
    chips, slots = owners // 2, owners * CAP
    in_vmem = pl.BlockSpec(memory_space=pltpu.VMEM)
    dma = pltpu.SemaphoreType.DMA
    return pl.pallas_call(
        functools.partial(block_kernel, owners),
        out_shape=jax.ShapeDtypeStruct((rows, D), BF16),
        in_specs=[pl.BlockSpec(memory_space=pltpu.HBM)] * 10,
        out_specs=in_vmem,
        scratch_shapes=[
            pltpu.VMEM((tokens, width), BF16),
            pltpu.VMEM((tokens, width), BF16),
            pltpu.VMEM((rows, D), BF16),
            pltpu.VMEM((2, rows), jnp.int32),
            pltpu.VMEM((2, rows), F32),
            pltpu.VMEM((width, D), BF16),
            pltpu.VMEM((units, HALF), BF16),
            pltpu.VMEM((units, HALF), BF16),
            pltpu.VMEM((units, HALF), BF16),
            pltpu.VMEM((tokens, width), BF16),
            pltpu.VMEM((tokens, width), BF16),
            pltpu.VMEM((tokens, width), BF16),
            pltpu.VMEM((chips * rows, width), BF16),
            pltpu.VMEM((2, chips * rows, HALF), BF16),
            pltpu.VMEM((2, chips * rows, HALF), BF16),
            pltpu.VMEM((chips * rows, HALF), F32),
            pltpu.VMEM((2, chips - 1, rows, HALF), BF16),
            pltpu.VMEM((2, chips - 1, rows, HALF), BF16),
            pltpu.VMEM((rows, D), F32),
            pltpu.VMEM((2, owners, CAP, HALF), BF16),
            pltpu.VMEM((2, owners, CAP, HALF), BF16),
            pltpu.VMEM((2, slots, units), BF16),
            pltpu.VMEM((2, slots, units), BF16),
            pltpu.VMEM((slots, units), BF16),
            pltpu.VMEM((slots, units), BF16),
            pltpu.VMEM((2, owners, CAP, HALF), BF16),
            pltpu.VMEM((2, owners, CAP, HALF), BF16),
            dma((9,)),
            dma((owners,)),
            dma((2,)),
            dma((2,)),
            dma((2,)),
            dma((2,)),
            dma((2, chips - 1)),
            dma((2, chips - 1)),
            dma((2, owners)),
            dma((2, owners)),
            dma((2,)),
            dma((2,)),
            dma,
            dma,
            dma((2, owners)),
            dma((2, owners)),
        ],
        compiler_params=pltpu.CompilerParams(
            collective_id=0, has_side_effects=True, vmem_limit_bytes=64 * 1024 * 1024
        ),
    )(
        queries,
        keys,
        values,
        out_weight,
        residual_in,
        gate_weight[0].T,
        up_weight[0].T,
        down_weight[0],
        expert_ids.T,
        route_gates.T,
    )


def solution(mesh):
    if mesh.shape["ctx"] == 2 and mesh.shape["exp"] % 2 == 0:
        body = functools.partial(per_device_pair, mesh.shape["exp"])
    else:
        body = per_device
    return jax.shard_map(
        body,
        mesh=mesh,
        in_specs=(
            P(("group", "ctx"), "exp"),
            P(("group", "ctx"), "exp"),
            P(("group", "ctx"), "exp"),
            P("exp", None),
            P(("group", "ctx", "exp"), None),
            P("exp", "ctx", None),
            P("exp", "ctx", None),
            P("exp", None, "ctx"),
            P(("group", "ctx", "exp"), None),
            P(("group", "ctx", "exp"), None),
        ),
        out_specs=P(("group", "ctx", "exp"), None),
        check_vma=False,
    )
```

```python
import functools

import jax
import jax.numpy as jnp
from jax import lax
from jax.experimental import pallas as pl
from jax.experimental.pallas import tpu as pltpu
from jax.sharding import PartitionSpec as P

D = 2048
HEAD_DIM = 128
CAP = 16


def per_device(
    queries,
    keys,
    values,
    out_weight,
    residual_in,
    gate_weight,
    up_weight,
    down_weight,
    expert_ids,
    route_gates,
):
    scale = HEAD_DIM ** (-0.5)
    local_tokens = queries.shape[0]
    head_count = queries.shape[1] // HEAD_DIM
    query_heads = queries.reshape(local_tokens, head_count, HEAD_DIM)
    key_piece = lax.all_gather(keys, "ctx", axis=0, tiled=True)
    value_piece = lax.all_gather(values, "ctx", axis=0, tiled=True)
    count = key_piece.shape[0]
    key_heads = key_piece.reshape(count, head_count, HEAD_DIM)
    value_heads = value_piece.reshape(count, head_count, HEAD_DIM)
    running_max = jnp.full((head_count, local_tokens), -1e30, jnp.float32)
    scores = (
        jnp.einsum("qhd,khd->hqk", query_heads, key_heads, preferred_element_type=jnp.float32)
        * scale
    )
    newest_max = jnp.maximum(running_max, jnp.max(scores, axis=2))
    weights = jnp.exp(scores - newest_max[:, :, None])
    numerator = jnp.einsum(
        "hqk,khd->hqd",
        weights.astype(jnp.bfloat16),
        value_heads,
        preferred_element_type=jnp.float32,
    )
    denominator = jnp.sum(weights, axis=2)
    final_max, numerator, denominator = (newest_max, numerator, denominator)
    attention = (numerator / denominator[:, :, None]).astype(jnp.bfloat16)
    attention = jnp.transpose(attention, (1, 0, 2)).reshape(local_tokens, head_count * HEAD_DIM)
    own_rows = residual_in.shape[0]
    hidden = residual_in.astype(jnp.float32) + lax.psum_scatter(
        jnp.dot(attention, out_weight, preferred_element_type=jnp.float32).astype(jnp.bfloat16),
        "exp",
        scatter_dimension=0,
        tiled=True,
    ).astype(jnp.float32)
    normed = (hidden * lax.rsqrt(jnp.mean(hidden * hidden, axis=1, keepdims=True) + 1e-06)).astype(
        jnp.bfloat16
    )
    owners = lax.axis_size("exp")
    flat_ids = expert_ids.reshape(-1)
    one_hot = (flat_ids[:, None] == jnp.arange(owners, dtype=jnp.int32)[None, :]).astype(jnp.int32)
    earlier = jnp.cumsum(one_hot, axis=0) - one_hot
    slot_index = jnp.sum(earlier * one_hot, axis=1)
    target = flat_ids * CAP + slot_index
    dispatch_table = (target[None, :] == jnp.arange(owners * CAP, dtype=jnp.int32)[:, None]).astype(
        jnp.bfloat16
    )
    routed = jnp.repeat(normed, 2, axis=0)
    outgoing = jnp.dot(dispatch_table, routed, preferred_element_type=jnp.float32).astype(
        jnp.bfloat16
    )
    incoming = lax.all_to_all(
        outgoing.reshape(owners, CAP, D), "exp", split_axis=0, concat_axis=0, tiled=True
    )
    slot_rows = incoming.reshape(owners * CAP, D)
    gate_part = jnp.dot(
        slot_rows,
        lax.all_gather(gate_weight[0], "ctx", axis=0, tiled=True),
        preferred_element_type=jnp.float32,
    )
    up_part = jnp.dot(
        slot_rows,
        lax.all_gather(up_weight[0], "ctx", axis=0, tiled=True),
        preferred_element_type=jnp.float32,
    )
    activation = (jax.nn.silu(gate_part) * up_part).astype(jnp.bfloat16)
    expert_result = jnp.dot(
        activation,
        lax.all_gather(down_weight[0], "ctx", axis=1, tiled=True),
        preferred_element_type=jnp.float32,
    ).astype(jnp.bfloat16)
    returned = lax.all_to_all(
        expert_result.reshape(owners, CAP, D), "exp", split_axis=0, concat_axis=0, tiled=True
    )
    per_route = jnp.einsum(
        "sr,sd->rd",
        dispatch_table,
        returned.reshape(owners * CAP, D),
        preferred_element_type=jnp.float32,
    )
    per_route = per_route.reshape(own_rows, 2, D)
    combined = per_route[:, 0, :] * route_gates[:, 0:1] + per_route[:, 1, :] * route_gates[:, 1:2]
    return (hidden + combined).astype(jnp.bfloat16)


F32 = jnp.float32
BF16 = jnp.bfloat16
HALF = D // 2


def dot(a, b):
    return jnp.dot(a, b, preferred_element_type=F32)


def block_kernel(
    owners,
    q_hbm,
    k_hbm,
    v_hbm,
    wo_hbm,
    res_hbm,
    wg_hbm,
    wu_hbm,
    wd_hbm,
    ids_hbm,
    gates_hbm,
    out_ref,
    k_ref,
    v_ref,
    res_ref,
    ids_ref,
    gates_ref,
    wo,
    wg,
    wu,
    wd,
    k_other,
    v_other,
    q_sorted,
    attn,
    mate_out,
    mate_in,
    own_part,
    reduce_out,
    reduce_in,
    hidden,
    outgoing,
    slab,
    part_out,
    part_in,
    act_own,
    act_other,
    results,
    returned,
    load_sem,
    q_sem,
    kv_send,
    kv_recv,
    mate_send,
    mate_recv,
    red_send,
    red_recv,
    disp_send,
    disp_recv,
    part_send,
    part_recv,
    act_send,
    act_recv,
    ret_send,
    ret_recv,
):
    chips = owners // 2
    ctx = lax.axis_index("ctx")
    exp = lax.axis_index("exp")
    chip, core = exp // 2, lax.rem(exp, 2)
    rows = res_ref.shape[0]
    slots = owners * CAP
    group_rows = chips * rows
    other_ctx = 1 - ctx

    def place(dc, de):
        return {
            "ctx": other_ctx if dc else ctx,
            "exp": lax.rem(exp + de, owners) if de else exp,
        }

    def dot_t(a, b):
        return lax.dot_general(a, b, (((1,), (1,)), ((), ())), preferred_element_type=F32)

    def remote(src, dst, send, recv, where):
        copy = pltpu.make_async_remote_copy(
            src_ref=src,
            dst_ref=dst,
            send_sem=send,
            recv_sem=recv,
            device_id=where,
            device_id_type=pl.DeviceIdType.MESH,
        )
        copy.start()
        return copy

    def load(n, src, dst):
        copy = pltpu.make_async_copy(src, dst, load_sem.at[n])
        copy.start()
        return copy

    q_loads = []
    for n in range(owners):
        keeper = core if n >= chips else 1 - core
        start = pl.multiple_of((2 * (n % chips) + keeper) * rows, rows)
        copy = pltpu.make_async_copy(
            q_hbm.at[pl.ds(start, rows), :], q_sorted.at[pl.ds(n * rows, rows), :], q_sem.at[n]
        )
        copy.start()
        q_loads.append(copy)
    k_load = load(0, k_hbm, k_ref)
    v_load = load(1, v_hbm, v_ref)
    ids_load = load(2, ids_hbm, ids_ref)
    gates_load = load(3, gates_hbm, gates_ref)
    wo_load = load(4, wo_hbm, wo)
    res_load = load(5, res_hbm, res_ref)
    wg_load = load(6, wg_hbm, wg)
    wu_load = load(7, wu_hbm, wu)
    wd_load = load(8, wd_hbm, wd)

    partners = [(dc, de) for dc in range(2) for de in range(owners) if dc or de]
    barrier = pltpu.get_barrier_semaphore()
    for dc, de in partners:
        pl.semaphore_signal(
            barrier, inc=1, device_id=place(dc, de), device_id_type=pl.DeviceIdType.MESH
        )
    pl.semaphore_wait(barrier, len(partners))

    across = place(1, 0)
    k_copy = remote(k_hbm, k_other, kv_send.at[0], kv_recv.at[0], across)
    v_copy = remote(v_hbm, v_other, kv_send.at[1], kv_recv.at[1], across)

    ids_load.wait()
    gates_load.wait()
    line = lax.broadcasted_iota(jnp.int32, (slots, rows), 0)
    picks = []
    for k in range(2):
        rel = ids_ref[k : k + 1, :] - exp
        picks.append(jnp.where(rel < 0, rel + owners, rel))
    named = [jnp.where(line == rel, 1.0, 0.0) for rel in picks]
    down_row = lax.broadcasted_iota(jnp.int32, (rows, rows), 0)
    down_col = lax.broadcasted_iota(jnp.int32, (rows, rows), 1)
    before = jnp.where(down_row < down_col, 1.0, 0.0)
    same = jnp.where(down_row == down_col, 1.0, 0.0)
    earlier = dot((named[0] + named[1]).astype(BF16), before.astype(BF16))
    tables = []
    for k in range(2):
        slot = jnp.sum(earlier * named[k], axis=0, keepdims=True)
        target = picks[k].astype(F32) * CAP + slot
        tables.append(jnp.where(line.astype(F32) == target, 1.0, 0.0))
    dispatch_t = (tables[0] + tables[1]).astype(BF16)
    combine = jnp.concatenate([table.T for table in tables], 0).astype(BF16)
    gate_columns = [
        jnp.sum(same * gates_ref[k : k + 1, :], axis=1, keepdims=True) for k in range(2)
    ]

    scale = HEAD_DIM ** (-0.5)
    head_count = q_sorted.shape[1] // HEAD_DIM

    def scores_of(h, keys):
        cols = pl.ds(h * HEAD_DIM, HEAD_DIM)
        return dot_t(q_sorted[:, cols], keys[:, cols]) * scale

    for copy in q_loads:
        copy.wait()
    k_load.wait()
    v_load.wait()
    wo_load.wait()
    near_scores = [scores_of(h, k_ref) for h in range(head_count)]
    near_tops = [jnp.max(near, axis=1, keepdims=True) for near in near_scores]
    k_copy.wait_recv()
    softmax = []
    for h in range(head_count):
        far = scores_of(h, k_other)
        top = jnp.maximum(near_tops[h], jnp.max(far, axis=1, keepdims=True))
        near, far = jnp.exp(near_scores[h] - top), jnp.exp(far - top)
        total = jnp.sum(near, axis=1, keepdims=True) + jnp.sum(far, axis=1, keepdims=True)
        cols = pl.ds(h * HEAD_DIM, HEAD_DIM)
        softmax.append((dot(near.astype(BF16), v_ref[:, cols]), far.astype(BF16), total))
    v_copy.wait_recv()
    for h in range(head_count):
        cols = pl.ds(h * HEAD_DIM, HEAD_DIM)
        numerator, far, total = softmax[h]
        attn[:, cols] = ((numerator + dot(far, v_other[:, cols])) / total).astype(BF16)

    mate = {"ctx": ctx, "exp": exp + 1 - 2 * core}
    mate_copies = []
    for c in range(2):
        mate_out[c] = dot(attn[:group_rows, :], wo[:, c * HALF : (c + 1) * HALF]).astype(BF16)
        mate_copies.append(
            remote(mate_out.at[c], mate_in.at[c], mate_send.at[c], mate_recv.at[c], mate)
        )
    red_copies = []
    own_start = pl.multiple_of(chip * rows, rows)
    res_load.wait()
    for c in range(2):
        cols = pl.ds(c * HALF, HALF)
        own_part[...] = dot(attn[group_rows:, :], wo[:, cols])
        mate_copies[c].wait_recv()
        for dz in range(chips - 1, 0, -1):
            to_chip = lax.rem(chip + dz, chips)
            start = pl.multiple_of(to_chip * rows, rows)
            reduce_out[c, dz - 1] = (
                own_part[pl.ds(start, rows), :] + mate_in[c, pl.ds(start, rows), :].astype(F32)
            ).astype(BF16)
            red_copies.append(
                remote(
                    reduce_out.at[c, dz - 1],
                    reduce_in.at[c, dz - 1],
                    red_send.at[c, dz - 1],
                    red_recv.at[c, dz - 1],
                    {"ctx": ctx, "exp": 2 * to_chip + core},
                )
            )
        hidden[:, cols] = (
            res_ref[:, cols].astype(F32)
            + own_part[pl.ds(own_start, rows), :]
            + mate_in[c, pl.ds(own_start, rows), :].astype(F32)
        )
    for c in range(2):
        cols = pl.ds(c * HALF, HALF)
        for dz in range(chips - 1, 0, -1):
            red_copies[c * (chips - 1) + chips - 1 - dz].wait_recv()
            hidden[:, cols] += reduce_in[c, dz - 1].astype(F32)

    square = jnp.mean(hidden[...] * hidden[...], axis=1, keepdims=True)
    normed = (hidden[...] * lax.rsqrt(square + 1e-06)).astype(BF16)
    for c in range(2):
        sent = dot(dispatch_t, normed[:, c * HALF : (c + 1) * HALF]).astype(BF16)
        outgoing[c] = sent.reshape(owners, CAP, HALF)
    disp_copies = {}
    order = sorted(partners, key=lambda p: (-p[0], abs(p[1] - owners // 2)))
    for dc, de in order:
        disp_copies[dc, de] = remote(
            outgoing.at[other_ctx if dc else ctx, de],
            slab.at[dc, de],
            disp_send.at[dc, de],
            disp_recv.at[dc, de],
            place(dc, de),
        )
    slab[0, 0] = outgoing[ctx, 0]
    for de in range(owners):
        disp_copies[1, de].wait_recv()
    wg_load.wait()
    wu_load.wait()
    far_rows = slab[1].reshape(slots, HALF)
    part_copies = []
    for n, weight in enumerate((wg, wu)):
        part_out[n] = dot_t(far_rows, weight[...]).astype(BF16)
        part_copies.append(
            remote(part_out.at[n], part_in.at[n], part_send.at[n], part_recv.at[n], across)
        )
    for de in range(1, owners):
        disp_copies[0, de].wait_recv()
    near_rows = slab[0].reshape(slots, HALF)
    gate_part = dot_t(near_rows, wg[...])
    up_part = dot_t(near_rows, wu[...])
    part_copies[0].wait_recv()
    gate_part = gate_part + part_in[0].astype(F32)
    gate_part = gate_part / (1.0 + jnp.exp(-gate_part))
    part_copies[1].wait_recv()
    act_own[...] = (gate_part * (up_part + part_in[1].astype(F32))).astype(BF16)
    act_copy = remote(act_own, act_other, act_send, act_recv, across)
    wd_load.wait()
    ret_copies = {}
    for dc in range(2):
        if dc:
            act_copy.wait_recv()
        result = dot((act_other if dc else act_own)[...], wd[...]).astype(BF16)
        results[dc] = result.reshape(owners, CAP, HALF)
        for de in sorted(range(owners), key=lambda e: abs(e - owners // 2)):
            if dc or de:
                ret_copies[dc, de] = remote(
                    results.at[dc, de],
                    returned.at[dc, de],
                    ret_send.at[dc, de],
                    ret_recv.at[dc, de],
                    place(dc, owners - de if de else 0),
                )
    returned[0, 0] = results[0, 0]
    for dc in range(2):
        for de in range(owners):
            if dc or de:
                ret_copies[dc, de].wait_recv()
        per_route = dot(combine, returned[dc].reshape(slots, HALF))
        cols = pl.ds(pl.multiple_of((other_ctx if dc else ctx) * HALF, HALF), HALF)
        out_ref[:, cols] = (
            hidden[:, cols]
            + per_route[:rows] * gate_columns[0]
            + per_route[rows:] * gate_columns[1]
        ).astype(BF16)

    for copy in (
        [k_copy, v_copy, act_copy]
        + mate_copies
        + red_copies
        + part_copies
        + list(disp_copies.values())
        + list(ret_copies.values())
    ):
        copy.wait_send()


def per_device_pair(
    owners,
    queries,
    keys,
    values,
    out_weight,
    residual_in,
    gate_weight,
    up_weight,
    down_weight,
    expert_ids,
    route_gates,
):
    tokens, width = queries.shape
    rows = residual_in.shape[0]
    units = gate_weight.shape[2]
    chips, slots = owners // 2, owners * CAP
    in_vmem = pl.BlockSpec(memory_space=pltpu.VMEM)
    dma = pltpu.SemaphoreType.DMA
    return pl.pallas_call(
        functools.partial(block_kernel, owners),
        out_shape=jax.ShapeDtypeStruct((rows, D), BF16),
        in_specs=[pl.BlockSpec(memory_space=pltpu.HBM)] * 10,
        out_specs=in_vmem,
        scratch_shapes=[
            pltpu.VMEM((tokens, width), BF16),
            pltpu.VMEM((tokens, width), BF16),
            pltpu.VMEM((rows, D), BF16),
            pltpu.VMEM((2, rows), jnp.int32),
            pltpu.VMEM((2, rows), F32),
            pltpu.VMEM((width, D), BF16),
            pltpu.VMEM((units, HALF), BF16),
            pltpu.VMEM((units, HALF), BF16),
            pltpu.VMEM((units, HALF), BF16),
            pltpu.VMEM((tokens, width), BF16),
            pltpu.VMEM((tokens, width), BF16),
            pltpu.VMEM((tokens, width), BF16),
            pltpu.VMEM((tokens, width), BF16),
            pltpu.VMEM((2, chips * rows, HALF), BF16),
            pltpu.VMEM((2, chips * rows, HALF), BF16),
            pltpu.VMEM((chips * rows, HALF), F32),
            pltpu.VMEM((2, chips - 1, rows, HALF), BF16),
            pltpu.VMEM((2, chips - 1, rows, HALF), BF16),
            pltpu.VMEM((rows, D), F32),
            pltpu.VMEM((2, owners, CAP, HALF), BF16),
            pltpu.VMEM((2, owners, CAP, HALF), BF16),
            pltpu.VMEM((2, slots, units), BF16),
            pltpu.VMEM((2, slots, units), BF16),
            pltpu.VMEM((slots, units), BF16),
            pltpu.VMEM((slots, units), BF16),
            pltpu.VMEM((2, owners, CAP, HALF), BF16),
            pltpu.VMEM((2, owners, CAP, HALF), BF16),
            dma((9,)),
            dma((owners,)),
            dma((2,)),
            dma((2,)),
            dma((2,)),
            dma((2,)),
            dma((2, chips - 1)),
            dma((2, chips - 1)),
            dma((2, owners)),
            dma((2, owners)),
            dma((2,)),
            dma((2,)),
            dma,
            dma,
            dma((2, owners)),
            dma((2, owners)),
        ],
        compiler_params=pltpu.CompilerParams(
            collective_id=0, has_side_effects=True, vmem_limit_bytes=64 * 1024 * 1024
        ),
    )(
        queries,
        keys,
        values,
        out_weight,
        residual_in,
        gate_weight[0].T,
        up_weight[0].T,
        down_weight[0],
        expert_ids.T,
        route_gates.T,
    )


def solution(mesh):
    if mesh.shape["ctx"] == 2 and mesh.shape["exp"] % 2 == 0:
        body = functools.partial(per_device_pair, mesh.shape["exp"])
    else:
        body = per_device
    return jax.shard_map(
        body,
        mesh=mesh,
        in_specs=(
            P(("group", "ctx"), "exp"),
            P(("group", "ctx"), "exp"),
            P(("group", "ctx"), "exp"),
            P("exp", None),
            P(("group", "ctx", "exp"), None),
            P("exp", "ctx", None),
            P("exp", "ctx", None),
            P("exp", None, "ctx"),
            P(("group", "ctx", "exp"), None),
            P(("group", "ctx", "exp"), None),
        ),
        out_specs=P(("group", "ctx", "exp"), None),
        check_vma=False,
    )
```

```python
import functools

import jax
import jax.numpy as jnp
from jax import lax
from jax.experimental import pallas as pl
from jax.experimental.pallas import tpu as pltpu
from jax.sharding import PartitionSpec as P

D = 2048
HEAD_DIM = 128
CAP = 16


def per_device(
    queries,
    keys,
    values,
    out_weight,
    residual_in,
    gate_weight,
    up_weight,
    down_weight,
    expert_ids,
    route_gates,
):
    scale = HEAD_DIM ** (-0.5)
    local_tokens = queries.shape[0]
    head_count = queries.shape[1] // HEAD_DIM
    query_heads = queries.reshape(local_tokens, head_count, HEAD_DIM)
    key_piece = lax.all_gather(keys, "ctx", axis=0, tiled=True)
    value_piece = lax.all_gather(values, "ctx", axis=0, tiled=True)
    count = key_piece.shape[0]
    key_heads = key_piece.reshape(count, head_count, HEAD_DIM)
    value_heads = value_piece.reshape(count, head_count, HEAD_DIM)
    running_max = jnp.full((head_count, local_tokens), -1e30, jnp.float32)
    scores = (
        jnp.einsum("qhd,khd->hqk", query_heads, key_heads, preferred_element_type=jnp.float32)
        * scale
    )
    newest_max = jnp.maximum(running_max, jnp.max(scores, axis=2))
    weights = jnp.exp(scores - newest_max[:, :, None])
    numerator = jnp.einsum(
        "hqk,khd->hqd",
        weights.astype(jnp.bfloat16),
        value_heads,
        preferred_element_type=jnp.float32,
    )
    denominator = jnp.sum(weights, axis=2)
    final_max, numerator, denominator = (newest_max, numerator, denominator)
    attention = (numerator / denominator[:, :, None]).astype(jnp.bfloat16)
    attention = jnp.transpose(attention, (1, 0, 2)).reshape(local_tokens, head_count * HEAD_DIM)
    own_rows = residual_in.shape[0]
    hidden = residual_in.astype(jnp.float32) + lax.psum_scatter(
        jnp.dot(attention, out_weight, preferred_element_type=jnp.float32).astype(jnp.bfloat16),
        "exp",
        scatter_dimension=0,
        tiled=True,
    ).astype(jnp.float32)
    normed = (hidden * lax.rsqrt(jnp.mean(hidden * hidden, axis=1, keepdims=True) + 1e-06)).astype(
        jnp.bfloat16
    )
    owners = lax.axis_size("exp")
    flat_ids = expert_ids.reshape(-1)
    one_hot = (flat_ids[:, None] == jnp.arange(owners, dtype=jnp.int32)[None, :]).astype(jnp.int32)
    earlier = jnp.cumsum(one_hot, axis=0) - one_hot
    slot_index = jnp.sum(earlier * one_hot, axis=1)
    target = flat_ids * CAP + slot_index
    dispatch_table = (target[None, :] == jnp.arange(owners * CAP, dtype=jnp.int32)[:, None]).astype(
        jnp.bfloat16
    )
    routed = jnp.repeat(normed, 2, axis=0)
    outgoing = jnp.dot(dispatch_table, routed, preferred_element_type=jnp.float32).astype(
        jnp.bfloat16
    )
    incoming = lax.all_to_all(
        outgoing.reshape(owners, CAP, D), "exp", split_axis=0, concat_axis=0, tiled=True
    )
    slot_rows = incoming.reshape(owners * CAP, D)
    gate_part = jnp.dot(
        slot_rows,
        lax.all_gather(gate_weight[0], "ctx", axis=0, tiled=True),
        preferred_element_type=jnp.float32,
    )
    up_part = jnp.dot(
        slot_rows,
        lax.all_gather(up_weight[0], "ctx", axis=0, tiled=True),
        preferred_element_type=jnp.float32,
    )
    activation = (jax.nn.silu(gate_part) * up_part).astype(jnp.bfloat16)
    expert_result = jnp.dot(
        activation,
        lax.all_gather(down_weight[0], "ctx", axis=1, tiled=True),
        preferred_element_type=jnp.float32,
    ).astype(jnp.bfloat16)
    returned = lax.all_to_all(
        expert_result.reshape(owners, CAP, D), "exp", split_axis=0, concat_axis=0, tiled=True
    )
    per_route = jnp.einsum(
        "sr,sd->rd",
        dispatch_table,
        returned.reshape(owners * CAP, D),
        preferred_element_type=jnp.float32,
    )
    per_route = per_route.reshape(own_rows, 2, D)
    combined = per_route[:, 0, :] * route_gates[:, 0:1] + per_route[:, 1, :] * route_gates[:, 1:2]
    return (hidden + combined).astype(jnp.bfloat16)


F32 = jnp.float32
BF16 = jnp.bfloat16
HALF = D // 2


def dot(a, b):
    return jnp.dot(a, b, preferred_element_type=F32)


def block_kernel(
    owners,
    q_hbm,
    k_hbm,
    v_hbm,
    wo_hbm,
    res_hbm,
    wg_hbm,
    wu_hbm,
    wd_hbm,
    ids_hbm,
    gates_hbm,
    out_ref,
    k_ref,
    v_ref,
    res_ref,
    ids_ref,
    gates_ref,
    wo,
    wg,
    wu,
    wd,
    k_other,
    v_other,
    q_sorted,
    attn,
    mate_out,
    mate_in,
    own_part,
    reduce_out,
    reduce_in,
    hidden,
    normed_halves,
    outgoing,
    slab,
    part_out,
    part_in,
    act_own,
    act_other,
    results,
    returned,
    load_sem,
    q_sem,
    kv_send,
    kv_recv,
    mate_send,
    mate_recv,
    red_send,
    red_recv,
    disp_send,
    disp_recv,
    part_send,
    part_recv,
    act_send,
    act_recv,
    ret_send,
    ret_recv,
):
    chips = owners // 2
    ctx = lax.axis_index("ctx")
    exp = lax.axis_index("exp")
    chip, core = exp // 2, lax.rem(exp, 2)
    rows = res_ref.shape[0]
    slots = owners * CAP
    group_rows = chips * rows
    other_ctx = 1 - ctx

    def place(dc, de):
        return {
            "ctx": other_ctx if dc else ctx,
            "exp": lax.rem(exp + de, owners) if de else exp,
        }

    def dot_t(a, b):
        return lax.dot_general(a, b, (((1,), (1,)), ((), ())), preferred_element_type=F32)

    def remote(src, dst, send, recv, where):
        copy = pltpu.make_async_remote_copy(
            src_ref=src,
            dst_ref=dst,
            send_sem=send,
            recv_sem=recv,
            device_id=where,
            device_id_type=pl.DeviceIdType.MESH,
        )
        copy.start()
        return copy

    def load(n, src, dst):
        copy = pltpu.make_async_copy(src, dst, load_sem.at[n])
        copy.start()
        return copy

    q_loads = []
    for n in range(owners):
        keeper = core if n >= chips else 1 - core
        start = pl.multiple_of((2 * (n % chips) + keeper) * rows, rows)
        copy = pltpu.make_async_copy(
            q_hbm.at[pl.ds(start, rows), :], q_sorted.at[pl.ds(n * rows, rows), :], q_sem.at[n]
        )
        copy.start()
        q_loads.append(copy)
    k_load = load(0, k_hbm, k_ref)
    v_load = load(1, v_hbm, v_ref)
    ids_load = load(2, ids_hbm, ids_ref)
    gates_load = load(3, gates_hbm, gates_ref)
    wo_load = load(4, wo_hbm, wo)
    res_load = load(5, res_hbm, res_ref)
    wg_load = load(6, wg_hbm, wg)
    wu_load = load(7, wu_hbm, wu)
    wd_load = load(8, wd_hbm, wd)

    partners = [(dc, de) for dc in range(2) for de in range(owners) if dc or de]
    barrier = pltpu.get_barrier_semaphore()
    for dc, de in partners:
        pl.semaphore_signal(
            barrier, inc=1, device_id=place(dc, de), device_id_type=pl.DeviceIdType.MESH
        )
    pl.semaphore_wait(barrier, len(partners))

    across = place(1, 0)
    k_copy = remote(k_hbm, k_other, kv_send.at[0], kv_recv.at[0], across)
    v_copy = remote(v_hbm, v_other, kv_send.at[1], kv_recv.at[1], across)

    ids_load.wait()
    gates_load.wait()
    line = lax.broadcasted_iota(jnp.int32, (slots, rows), 0)
    picks = []
    for k in range(2):
        rel = ids_ref[k : k + 1, :] - exp
        picks.append(jnp.where(rel < 0, rel + owners, rel))
    named = [jnp.where(line == rel, 1.0, 0.0) for rel in picks]
    down_row = lax.broadcasted_iota(jnp.int32, (rows, rows), 0)
    down_col = lax.broadcasted_iota(jnp.int32, (rows, rows), 1)
    before = jnp.where(down_row < down_col, 1.0, 0.0)
    same = jnp.where(down_row == down_col, 1.0, 0.0)
    earlier = dot((named[0] + named[1]).astype(BF16), before.astype(BF16))
    tables = []
    for k in range(2):
        slot = jnp.sum(earlier * named[k], axis=0, keepdims=True)
        target = picks[k].astype(F32) * CAP + slot
        tables.append(jnp.where(line.astype(F32) == target, 1.0, 0.0))
    dispatch_t = (tables[0] + tables[1]).astype(BF16)
    combine = jnp.concatenate([table.T for table in tables], 0).astype(BF16)
    gate_columns = [
        jnp.sum(same * gates_ref[k : k + 1, :], axis=1, keepdims=True) for k in range(2)
    ]

    scale = HEAD_DIM ** (-0.5)
    head_count = q_sorted.shape[1] // HEAD_DIM

    def scores_of(h, keys):
        cols = pl.ds(h * HEAD_DIM, HEAD_DIM)
        return dot_t(q_sorted[:, cols], keys[:, cols]) * scale

    for copy in q_loads:
        copy.wait()
    k_load.wait()
    v_load.wait()
    wo_load.wait()
    near_scores = [scores_of(h, k_ref) for h in range(head_count)]
    near_tops = [jnp.max(near, axis=1, keepdims=True) for near in near_scores]
    k_copy.wait_recv()
    softmax = []
    for h in range(head_count):
        far = scores_of(h, k_other)
        top = jnp.maximum(near_tops[h], jnp.max(far, axis=1, keepdims=True))
        near, far = jnp.exp(near_scores[h] - top), jnp.exp(far - top)
        total = jnp.sum(near, axis=1, keepdims=True) + jnp.sum(far, axis=1, keepdims=True)
        cols = pl.ds(h * HEAD_DIM, HEAD_DIM)
        softmax.append((dot(near.astype(BF16), v_ref[:, cols]), far.astype(BF16), total))
    v_copy.wait_recv()
    for h in range(head_count):
        cols = pl.ds(h * HEAD_DIM, HEAD_DIM)
        numerator, far, total = softmax[h]
        attn[:, cols] = ((numerator + dot(far, v_other[:, cols])) / total).astype(BF16)

    mate = {"ctx": ctx, "exp": exp + 1 - 2 * core}
    mate_copies = []
    for c in range(2):
        mate_out[c] = dot(attn[:group_rows, :], wo[:, c * HALF : (c + 1) * HALF]).astype(BF16)
        mate_copies.append(
            remote(mate_out.at[c], mate_in.at[c], mate_send.at[c], mate_recv.at[c], mate)
        )
    red_copies = []
    own_start = pl.multiple_of(chip * rows, rows)
    res_load.wait()
    for c in range(2):
        cols = pl.ds(c * HALF, HALF)
        own_part[...] = dot(attn[group_rows:, :], wo[:, cols])
        mate_copies[c].wait_recv()
        for dz in range(chips - 1, 0, -1):
            to_chip = lax.rem(chip + dz, chips)
            start = pl.multiple_of(to_chip * rows, rows)
            reduce_out[c, dz - 1] = (
                own_part[pl.ds(start, rows), :] + mate_in[c, pl.ds(start, rows), :].astype(F32)
            ).astype(BF16)
            red_copies.append(
                remote(
                    reduce_out.at[c, dz - 1],
                    reduce_in.at[c, dz - 1],
                    red_send.at[c, dz - 1],
                    red_recv.at[c, dz - 1],
                    {"ctx": ctx, "exp": 2 * to_chip + core},
                )
            )
        hidden[:, cols] = (
            res_ref[:, cols].astype(F32)
            + own_part[pl.ds(own_start, rows), :]
            + mate_in[c, pl.ds(own_start, rows), :].astype(F32)
        )
    for c in range(2):
        cols = pl.ds(c * HALF, HALF)
        for copy in red_copies[c * (chips - 1) : (c + 1) * (chips - 1)]:
            copy.wait_recv()
        total = hidden[:, cols]
        for dz in range(chips - 1, 0, -1):
            total = total + reduce_in[c, dz - 1].astype(F32)
        hidden[:, cols] = total

    square = jnp.mean(hidden[...] * hidden[...], axis=1, keepdims=True)
    normed = (hidden[...] * lax.rsqrt(square + 1e-06)).astype(BF16)
    for c in range(2):
        normed_halves[c] = normed[:, c * HALF : (c + 1) * HALF]
    disp_copies = {}
    for dc in (1, 0):
        c = other_ctx if dc else ctx
        outgoing[dc] = dot(dispatch_t, normed_halves[c]).astype(BF16).reshape(owners, CAP, HALF)
        for de in sorted(range(owners), key=lambda e: abs(e - owners // 2)):
            if dc or de:
                disp_copies[dc, de] = remote(
                    outgoing.at[dc, de],
                    slab.at[dc, de],
                    disp_send.at[dc, de],
                    disp_recv.at[dc, de],
                    place(dc, de),
                )
    slab[0, 0] = outgoing[0, 0]
    for de in range(owners):
        disp_copies[1, de].wait_recv()
    wg_load.wait()
    wu_load.wait()
    far_rows = slab[1].reshape(slots, HALF)
    part_copies = []
    for n, weight in enumerate((wg, wu)):
        part_out[n] = dot_t(far_rows, weight[...]).astype(BF16)
        part_copies.append(
            remote(part_out.at[n], part_in.at[n], part_send.at[n], part_recv.at[n], across)
        )
    for de in range(1, owners):
        disp_copies[0, de].wait_recv()
    near_rows = slab[0].reshape(slots, HALF)
    gate_part = dot_t(near_rows, wg[...])
    up_part = dot_t(near_rows, wu[...])
    part_copies[0].wait_recv()
    gate_part = gate_part + part_in[0].astype(F32)
    gate_part = gate_part / (1.0 + jnp.exp(-gate_part))
    part_copies[1].wait_recv()
    act_own[...] = (gate_part * (up_part + part_in[1].astype(F32))).astype(BF16)
    act_copy = remote(act_own, act_other, act_send, act_recv, across)
    wd_load.wait()
    ret_copies = {}
    for dc in range(2):
        if dc:
            act_copy.wait_recv()
        result = dot((act_other if dc else act_own)[...], wd[...]).astype(BF16)
        results[dc] = result.reshape(owners, CAP, HALF)
        for de in sorted(range(owners), key=lambda e: abs(e - owners // 2)):
            if dc or de:
                ret_copies[dc, de] = remote(
                    results.at[dc, de],
                    returned.at[dc, de],
                    ret_send.at[dc, de],
                    ret_recv.at[dc, de],
                    place(dc, owners - de if de else 0),
                )
    returned[0, 0] = results[0, 0]
    for dc in range(2):
        for de in range(owners):
            if dc or de:
                ret_copies[dc, de].wait_recv()
        per_route = dot(combine, returned[dc].reshape(slots, HALF))
        cols = pl.ds(pl.multiple_of((other_ctx if dc else ctx) * HALF, HALF), HALF)
        out_ref[:, cols] = (
            hidden[:, cols]
            + per_route[:rows] * gate_columns[0]
            + per_route[rows:] * gate_columns[1]
        ).astype(BF16)

    for copy in (
        [k_copy, v_copy, act_copy]
        + mate_copies
        + red_copies
        + part_copies
        + list(disp_copies.values())
        + list(ret_copies.values())
    ):
        copy.wait_send()


def per_device_pair(
    owners,
    queries,
    keys,
    values,
    out_weight,
    residual_in,
    gate_weight,
    up_weight,
    down_weight,
    expert_ids,
    route_gates,
):
    tokens, width = queries.shape
    rows = residual_in.shape[0]
    units = gate_weight.shape[2]
    chips, slots = owners // 2, owners * CAP
    in_vmem = pl.BlockSpec(memory_space=pltpu.VMEM)
    dma = pltpu.SemaphoreType.DMA
    return pl.pallas_call(
        functools.partial(block_kernel, owners),
        out_shape=jax.ShapeDtypeStruct((rows, D), BF16),
        in_specs=[pl.BlockSpec(memory_space=pltpu.HBM)] * 10,
        out_specs=in_vmem,
        scratch_shapes=[
            pltpu.VMEM((tokens, width), BF16),
            pltpu.VMEM((tokens, width), BF16),
            pltpu.VMEM((rows, D), BF16),
            pltpu.VMEM((2, rows), jnp.int32),
            pltpu.VMEM((2, rows), F32),
            pltpu.VMEM((width, D), BF16),
            pltpu.VMEM((units, HALF), BF16),
            pltpu.VMEM((units, HALF), BF16),
            pltpu.VMEM((units, HALF), BF16),
            pltpu.VMEM((tokens, width), BF16),
            pltpu.VMEM((tokens, width), BF16),
            pltpu.VMEM((tokens, width), BF16),
            pltpu.VMEM((tokens, width), BF16),
            pltpu.VMEM((2, chips * rows, HALF), BF16),
            pltpu.VMEM((2, chips * rows, HALF), BF16),
            pltpu.VMEM((chips * rows, HALF), F32),
            pltpu.VMEM((2, chips - 1, rows, HALF), BF16),
            pltpu.VMEM((2, chips - 1, rows, HALF), BF16),
            pltpu.VMEM((rows, D), F32),
            pltpu.VMEM((2, rows, HALF), BF16),
            pltpu.VMEM((2, owners, CAP, HALF), BF16),
            pltpu.VMEM((2, owners, CAP, HALF), BF16),
            pltpu.VMEM((2, slots, units), BF16),
            pltpu.VMEM((2, slots, units), BF16),
            pltpu.VMEM((slots, units), BF16),
            pltpu.VMEM((slots, units), BF16),
            pltpu.VMEM((2, owners, CAP, HALF), BF16),
            pltpu.VMEM((2, owners, CAP, HALF), BF16),
            dma((9,)),
            dma((owners,)),
            dma((2,)),
            dma((2,)),
            dma((2,)),
            dma((2,)),
            dma((2, chips - 1)),
            dma((2, chips - 1)),
            dma((2, owners)),
            dma((2, owners)),
            dma((2,)),
            dma((2,)),
            dma,
            dma,
            dma((2, owners)),
            dma((2, owners)),
        ],
        compiler_params=pltpu.CompilerParams(
            collective_id=0, has_side_effects=True, vmem_limit_bytes=64 * 1024 * 1024
        ),
    )(
        queries,
        keys,
        values,
        out_weight,
        residual_in,
        gate_weight[0].T,
        up_weight[0].T,
        down_weight[0],
        expert_ids.T,
        route_gates.T,
    )


def solution(mesh):
    if mesh.shape["ctx"] == 2 and mesh.shape["exp"] % 2 == 0:
        body = functools.partial(per_device_pair, mesh.shape["exp"])
    else:
        body = per_device
    return jax.shard_map(
        body,
        mesh=mesh,
        in_specs=(
            P(("group", "ctx"), "exp"),
            P(("group", "ctx"), "exp"),
            P(("group", "ctx"), "exp"),
            P("exp", None),
            P(("group", "ctx", "exp"), None),
            P("exp", "ctx", None),
            P("exp", "ctx", None),
            P("exp", None, "ctx"),
            P(("group", "ctx", "exp"), None),
            P(("group", "ctx", "exp"), None),
        ),
        out_specs=P(("group", "ctx", "exp"), None),
        check_vma=False,
    )
```

```python
import functools

import jax
import jax.numpy as jnp
from jax import lax
from jax.experimental import pallas as pl
from jax.experimental.pallas import tpu as pltpu
from jax.sharding import PartitionSpec as P

D = 2048
HEAD_DIM = 128
CAP = 16


def per_device(
    queries,
    keys,
    values,
    out_weight,
    residual_in,
    gate_weight,
    up_weight,
    down_weight,
    expert_ids,
    route_gates,
):
    scale = HEAD_DIM ** (-0.5)
    local_tokens = queries.shape[0]
    head_count = queries.shape[1] // HEAD_DIM
    query_heads = queries.reshape(local_tokens, head_count, HEAD_DIM)
    key_piece = lax.all_gather(keys, "ctx", axis=0, tiled=True)
    value_piece = lax.all_gather(values, "ctx", axis=0, tiled=True)
    count = key_piece.shape[0]
    key_heads = key_piece.reshape(count, head_count, HEAD_DIM)
    value_heads = value_piece.reshape(count, head_count, HEAD_DIM)
    running_max = jnp.full((head_count, local_tokens), -1e30, jnp.float32)
    scores = (
        jnp.einsum("qhd,khd->hqk", query_heads, key_heads, preferred_element_type=jnp.float32)
        * scale
    )
    newest_max = jnp.maximum(running_max, jnp.max(scores, axis=2))
    weights = jnp.exp(scores - newest_max[:, :, None])
    numerator = jnp.einsum(
        "hqk,khd->hqd",
        weights.astype(jnp.bfloat16),
        value_heads,
        preferred_element_type=jnp.float32,
    )
    denominator = jnp.sum(weights, axis=2)
    final_max, numerator, denominator = (newest_max, numerator, denominator)
    attention = (numerator / denominator[:, :, None]).astype(jnp.bfloat16)
    attention = jnp.transpose(attention, (1, 0, 2)).reshape(local_tokens, head_count * HEAD_DIM)
    own_rows = residual_in.shape[0]
    hidden = residual_in.astype(jnp.float32) + lax.psum_scatter(
        jnp.dot(attention, out_weight, preferred_element_type=jnp.float32).astype(jnp.bfloat16),
        "exp",
        scatter_dimension=0,
        tiled=True,
    ).astype(jnp.float32)
    normed = (hidden * lax.rsqrt(jnp.mean(hidden * hidden, axis=1, keepdims=True) + 1e-06)).astype(
        jnp.bfloat16
    )
    owners = lax.axis_size("exp")
    flat_ids = expert_ids.reshape(-1)
    one_hot = (flat_ids[:, None] == jnp.arange(owners, dtype=jnp.int32)[None, :]).astype(jnp.int32)
    earlier = jnp.cumsum(one_hot, axis=0) - one_hot
    slot_index = jnp.sum(earlier * one_hot, axis=1)
    target = flat_ids * CAP + slot_index
    dispatch_table = (target[None, :] == jnp.arange(owners * CAP, dtype=jnp.int32)[:, None]).astype(
        jnp.bfloat16
    )
    routed = jnp.repeat(normed, 2, axis=0)
    outgoing = jnp.dot(dispatch_table, routed, preferred_element_type=jnp.float32).astype(
        jnp.bfloat16
    )
    incoming = lax.all_to_all(
        outgoing.reshape(owners, CAP, D), "exp", split_axis=0, concat_axis=0, tiled=True
    )
    slot_rows = incoming.reshape(owners * CAP, D)
    gate_part = jnp.dot(
        slot_rows,
        lax.all_gather(gate_weight[0], "ctx", axis=0, tiled=True),
        preferred_element_type=jnp.float32,
    )
    up_part = jnp.dot(
        slot_rows,
        lax.all_gather(up_weight[0], "ctx", axis=0, tiled=True),
        preferred_element_type=jnp.float32,
    )
    activation = (jax.nn.silu(gate_part) * up_part).astype(jnp.bfloat16)
    expert_result = jnp.dot(
        activation,
        lax.all_gather(down_weight[0], "ctx", axis=1, tiled=True),
        preferred_element_type=jnp.float32,
    ).astype(jnp.bfloat16)
    returned = lax.all_to_all(
        expert_result.reshape(owners, CAP, D), "exp", split_axis=0, concat_axis=0, tiled=True
    )
    per_route = jnp.einsum(
        "sr,sd->rd",
        dispatch_table,
        returned.reshape(owners * CAP, D),
        preferred_element_type=jnp.float32,
    )
    per_route = per_route.reshape(own_rows, 2, D)
    combined = per_route[:, 0, :] * route_gates[:, 0:1] + per_route[:, 1, :] * route_gates[:, 1:2]
    return (hidden + combined).astype(jnp.bfloat16)


F32 = jnp.float32
BF16 = jnp.bfloat16
HALF = D // 2


def dot(a, b):
    return jnp.dot(a, b, preferred_element_type=F32)


def block_kernel(
    owners,
    q_hbm,
    k_hbm,
    v_hbm,
    wo_hbm,
    res_hbm,
    wg_hbm,
    wu_hbm,
    wd_hbm,
    ids_hbm,
    gates_hbm,
    out_ref,
    k_ref,
    v_ref,
    res_ref,
    ids_ref,
    gates_ref,
    wo,
    wg,
    wu,
    wd,
    k_other,
    v_other,
    q_sorted,
    attn,
    mate_out,
    mate_in,
    own_part,
    reduce_out,
    reduce_in,
    hidden,
    normed_halves,
    outgoing,
    slab,
    part_out,
    part_in,
    act_own,
    act_other,
    results,
    returned,
    load_sem,
    q_sem,
    kv_send,
    kv_recv,
    mate_send,
    mate_recv,
    red_send,
    red_recv,
    disp_send,
    disp_recv,
    part_send,
    part_recv,
    act_send,
    act_recv,
    ret_send,
    ret_recv,
):
    chips = owners // 2
    ctx = lax.axis_index("ctx")
    exp = lax.axis_index("exp")
    chip, core = exp // 2, lax.rem(exp, 2)
    rows = res_ref.shape[0]
    slots = owners * CAP
    group_rows = chips * rows
    other_ctx = 1 - ctx

    def place(dc, de):
        return {
            "ctx": other_ctx if dc else ctx,
            "exp": lax.rem(exp + de, owners) if de else exp,
        }

    def dot_t(a, b):
        return lax.dot_general(a, b, (((1,), (1,)), ((), ())), preferred_element_type=F32)

    def remote(src, dst, send, recv, where):
        copy = pltpu.make_async_remote_copy(
            src_ref=src,
            dst_ref=dst,
            send_sem=send,
            recv_sem=recv,
            device_id=where,
            device_id_type=pl.DeviceIdType.MESH,
        )
        copy.start()
        return copy

    def load(n, src, dst):
        copy = pltpu.make_async_copy(src, dst, load_sem.at[n])
        copy.start()
        return copy

    q_loads = []
    for n in range(owners):
        keeper = core if n >= chips else 1 - core
        start = pl.multiple_of((2 * (n % chips) + keeper) * rows, rows)
        copy = pltpu.make_async_copy(
            q_hbm.at[pl.ds(start, rows), :], q_sorted.at[pl.ds(n * rows, rows), :], q_sem.at[n]
        )
        copy.start()
        q_loads.append(copy)
    k_load = load(0, k_hbm, k_ref)
    v_load = load(1, v_hbm, v_ref)
    ids_load = load(2, ids_hbm, ids_ref)
    gates_load = load(3, gates_hbm, gates_ref)
    wo_load = load(4, wo_hbm, wo)
    res_load = load(5, res_hbm, res_ref)
    wg_load = load(6, wg_hbm, wg)
    wu_load = load(7, wu_hbm, wu)
    wd_load = load(8, wd_hbm, wd)

    partners = [(dc, de) for dc in range(2) for de in range(owners) if dc or de]
    barrier = pltpu.get_barrier_semaphore()
    for dc, de in partners:
        pl.semaphore_signal(
            barrier, inc=1, device_id=place(dc, de), device_id_type=pl.DeviceIdType.MESH
        )
    pl.semaphore_wait(barrier, len(partners))

    across = place(1, 0)
    k_copy = remote(k_hbm, k_other, kv_send.at[0], kv_recv.at[0], across)

    ids_load.wait()
    gates_load.wait()
    line = lax.broadcasted_iota(jnp.int32, (slots, rows), 0)
    picks = []
    for k in range(2):
        rel = ids_ref[k : k + 1, :] - exp
        picks.append(jnp.where(rel < 0, rel + owners, rel))
    named = [jnp.where(line == rel, 1.0, 0.0) for rel in picks]
    down_row = lax.broadcasted_iota(jnp.int32, (rows, rows), 0)
    down_col = lax.broadcasted_iota(jnp.int32, (rows, rows), 1)
    before = jnp.where(down_row < down_col, 1.0, 0.0)
    same = jnp.where(down_row == down_col, 1.0, 0.0)
    earlier = dot((named[0] + named[1]).astype(BF16), before.astype(BF16))
    tables = []
    for k in range(2):
        slot = jnp.sum(earlier * named[k], axis=0, keepdims=True)
        target = picks[k].astype(F32) * CAP + slot
        tables.append(jnp.where(line.astype(F32) == target, 1.0, 0.0))
    dispatch_t = (tables[0] + tables[1]).astype(BF16)
    combine = jnp.concatenate([table.T for table in tables], 0).astype(BF16)
    gate_columns = [
        jnp.sum(same * gates_ref[k : k + 1, :], axis=1, keepdims=True) for k in range(2)
    ]

    v_copy = remote(v_hbm, v_other, kv_send.at[1], kv_recv.at[1], across)

    scale = HEAD_DIM ** (-0.5)
    head_count = q_sorted.shape[1] // HEAD_DIM

    def scores_of(h, keys):
        cols = pl.ds(h * HEAD_DIM, HEAD_DIM)
        return dot_t(q_sorted[:, cols], keys[:, cols]) * scale

    for copy in q_loads:
        copy.wait()
    k_load.wait()
    v_load.wait()
    wo_load.wait()
    near_scores = [scores_of(h, k_ref) for h in range(head_count)]
    near_tops = [jnp.max(near, axis=1, keepdims=True) for near in near_scores]
    k_copy.wait_recv()
    softmax = []
    for h in range(head_count):
        far = scores_of(h, k_other)
        top = jnp.maximum(near_tops[h], jnp.max(far, axis=1, keepdims=True))
        near, far = jnp.exp(near_scores[h] - top), jnp.exp(far - top)
        total = jnp.sum(near, axis=1, keepdims=True) + jnp.sum(far, axis=1, keepdims=True)
        cols = pl.ds(h * HEAD_DIM, HEAD_DIM)
        softmax.append((dot(near.astype(BF16), v_ref[:, cols]), far.astype(BF16), total))
    v_copy.wait_recv()
    for h in range(head_count):
        cols = pl.ds(h * HEAD_DIM, HEAD_DIM)
        numerator, far, total = softmax[h]
        attn[:, cols] = ((numerator + dot(far, v_other[:, cols])) / total).astype(BF16)

    mate = {"ctx": ctx, "exp": exp + 1 - 2 * core}
    mate_copies = []
    for c in range(2):
        mate_out[c] = dot(attn[:group_rows, :], wo[:, c * HALF : (c + 1) * HALF]).astype(BF16)
        mate_copies.append(
            remote(mate_out.at[c], mate_in.at[c], mate_send.at[c], mate_recv.at[c], mate)
        )
    red_copies = []
    own_start = pl.multiple_of(chip * rows, rows)
    res_load.wait()
    for c in range(2):
        cols = pl.ds(c * HALF, HALF)
        own_part[...] = dot(attn[group_rows:, :], wo[:, cols])
        mate_copies[c].wait_recv()
        for dz in range(chips - 1, 0, -1):
            to_chip = lax.rem(chip + dz, chips)
            start = pl.multiple_of(to_chip * rows, rows)
            reduce_out[c, dz - 1] = (
                own_part[pl.ds(start, rows), :] + mate_in[c, pl.ds(start, rows), :].astype(F32)
            ).astype(BF16)
            red_copies.append(
                remote(
                    reduce_out.at[c, dz - 1],
                    reduce_in.at[c, dz - 1],
                    red_send.at[c, dz - 1],
                    red_recv.at[c, dz - 1],
                    {"ctx": ctx, "exp": 2 * to_chip + core},
                )
            )
        hidden[:, cols] = (
            res_ref[:, cols].astype(F32)
            + own_part[pl.ds(own_start, rows), :]
            + mate_in[c, pl.ds(own_start, rows), :].astype(F32)
        )
    for c in range(2):
        cols = pl.ds(c * HALF, HALF)
        for copy in red_copies[c * (chips - 1) : (c + 1) * (chips - 1)]:
            copy.wait_recv()
        total = hidden[:, cols]
        for dz in range(chips - 1, 0, -1):
            total = total + reduce_in[c, dz - 1].astype(F32)
        hidden[:, cols] = total

    square = jnp.mean(hidden[...] * hidden[...], axis=1, keepdims=True)
    normed = (hidden[...] * lax.rsqrt(square + 1e-06)).astype(BF16)
    for c in range(2):
        normed_halves[c] = normed[:, c * HALF : (c + 1) * HALF]
    disp_copies = {}
    for dc in (1, 0):
        c = other_ctx if dc else ctx
        outgoing[dc] = dot(dispatch_t, normed_halves[c]).astype(BF16).reshape(owners, CAP, HALF)
        for de in sorted(range(owners), key=lambda e: abs(e - owners // 2)):
            if dc or de:
                disp_copies[dc, de] = remote(
                    outgoing.at[dc, de],
                    slab.at[dc, de],
                    disp_send.at[dc, de],
                    disp_recv.at[dc, de],
                    place(dc, de),
                )
    slab[0, 0] = outgoing[0, 0]
    for de in range(owners):
        disp_copies[1, de].wait_recv()
    wg_load.wait()
    wu_load.wait()
    far_rows = slab[1].reshape(slots, HALF)
    part_copies = []
    for n, weight in enumerate((wg, wu)):
        part_out[n] = dot_t(far_rows, weight[...]).astype(BF16)
        part_copies.append(
            remote(part_out.at[n], part_in.at[n], part_send.at[n], part_recv.at[n], across)
        )
    for de in range(1, owners):
        disp_copies[0, de].wait_recv()
    near_rows = slab[0].reshape(slots, HALF)
    gate_part = dot_t(near_rows, wg[...])
    up_part = dot_t(near_rows, wu[...])
    part_copies[0].wait_recv()
    gate_part = gate_part + part_in[0].astype(F32)
    gate_part = gate_part / (1.0 + jnp.exp(-gate_part))
    part_copies[1].wait_recv()
    act_own[...] = (gate_part * (up_part + part_in[1].astype(F32))).astype(BF16)
    act_copy = remote(act_own, act_other, act_send, act_recv, across)
    wd_load.wait()
    ret_copies = {}
    for dc in range(2):
        if dc:
            act_copy.wait_recv()
        result = dot((act_other if dc else act_own)[...], wd[...]).astype(BF16)
        results[dc] = result.reshape(owners, CAP, HALF)
        for de in sorted(range(owners), key=lambda e: abs(e - owners // 2)):
            if dc or de:
                ret_copies[dc, de] = remote(
                    results.at[dc, de],
                    returned.at[dc, de],
                    ret_send.at[dc, de],
                    ret_recv.at[dc, de],
                    place(dc, owners - de if de else 0),
                )
    returned[0, 0] = results[0, 0]
    for dc in range(2):
        for de in range(owners):
            if dc or de:
                ret_copies[dc, de].wait_recv()
        per_route = dot(combine, returned[dc].reshape(slots, HALF))
        cols = pl.ds(pl.multiple_of((other_ctx if dc else ctx) * HALF, HALF), HALF)
        out_ref[:, cols] = (
            hidden[:, cols]
            + per_route[:rows] * gate_columns[0]
            + per_route[rows:] * gate_columns[1]
        ).astype(BF16)

    for copy in (
        [k_copy, v_copy, act_copy]
        + mate_copies
        + red_copies
        + part_copies
        + list(disp_copies.values())
        + list(ret_copies.values())
    ):
        copy.wait_send()


def per_device_pair(
    owners,
    queries,
    keys,
    values,
    out_weight,
    residual_in,
    gate_weight,
    up_weight,
    down_weight,
    expert_ids,
    route_gates,
):
    tokens, width = queries.shape
    rows = residual_in.shape[0]
    units = gate_weight.shape[2]
    chips, slots = owners // 2, owners * CAP
    in_vmem = pl.BlockSpec(memory_space=pltpu.VMEM)
    dma = pltpu.SemaphoreType.DMA
    return pl.pallas_call(
        functools.partial(block_kernel, owners),
        out_shape=jax.ShapeDtypeStruct((rows, D), BF16),
        in_specs=[pl.BlockSpec(memory_space=pltpu.HBM)] * 10,
        out_specs=in_vmem,
        scratch_shapes=[
            pltpu.VMEM((tokens, width), BF16),
            pltpu.VMEM((tokens, width), BF16),
            pltpu.VMEM((rows, D), BF16),
            pltpu.VMEM((2, rows), jnp.int32),
            pltpu.VMEM((2, rows), F32),
            pltpu.VMEM((width, D), BF16),
            pltpu.VMEM((units, HALF), BF16),
            pltpu.VMEM((units, HALF), BF16),
            pltpu.VMEM((units, HALF), BF16),
            pltpu.VMEM((tokens, width), BF16),
            pltpu.VMEM((tokens, width), BF16),
            pltpu.VMEM((tokens, width), BF16),
            pltpu.VMEM((tokens, width), BF16),
            pltpu.VMEM((2, chips * rows, HALF), BF16),
            pltpu.VMEM((2, chips * rows, HALF), BF16),
            pltpu.VMEM((chips * rows, HALF), F32),
            pltpu.VMEM((2, chips - 1, rows, HALF), BF16),
            pltpu.VMEM((2, chips - 1, rows, HALF), BF16),
            pltpu.VMEM((rows, D), F32),
            pltpu.VMEM((2, rows, HALF), BF16),
            pltpu.VMEM((2, owners, CAP, HALF), BF16),
            pltpu.VMEM((2, owners, CAP, HALF), BF16),
            pltpu.VMEM((2, slots, units), BF16),
            pltpu.VMEM((2, slots, units), BF16),
            pltpu.VMEM((slots, units), BF16),
            pltpu.VMEM((slots, units), BF16),
            pltpu.VMEM((2, owners, CAP, HALF), BF16),
            pltpu.VMEM((2, owners, CAP, HALF), BF16),
            dma((9,)),
            dma((owners,)),
            dma((2,)),
            dma((2,)),
            dma((2,)),
            dma((2,)),
            dma((2, chips - 1)),
            dma((2, chips - 1)),
            dma((2, owners)),
            dma((2, owners)),
            dma((2,)),
            dma((2,)),
            dma,
            dma,
            dma((2, owners)),
            dma((2, owners)),
        ],
        compiler_params=pltpu.CompilerParams(
            collective_id=0, has_side_effects=True, vmem_limit_bytes=64 * 1024 * 1024
        ),
    )(
        queries,
        keys,
        values,
        out_weight,
        residual_in,
        gate_weight[0].T,
        up_weight[0].T,
        down_weight[0],
        expert_ids.T,
        route_gates.T,
    )


def solution(mesh):
    if mesh.shape["ctx"] == 2 and mesh.shape["exp"] % 2 == 0:
        body = functools.partial(per_device_pair, mesh.shape["exp"])
    else:
        body = per_device
    return jax.shard_map(
        body,
        mesh=mesh,
        in_specs=(
            P(("group", "ctx"), "exp"),
            P(("group", "ctx"), "exp"),
            P(("group", "ctx"), "exp"),
            P("exp", None),
            P(("group", "ctx", "exp"), None),
            P("exp", "ctx", None),
            P("exp", "ctx", None),
            P("exp", None, "ctx"),
            P(("group", "ctx", "exp"), None),
            P(("group", "ctx", "exp"), None),
        ),
        out_specs=P(("group", "ctx", "exp"), None),
        check_vma=False,
    )
```

```python
import functools

import jax
import jax.numpy as jnp
from jax import lax
from jax.experimental import pallas as pl
from jax.experimental.pallas import tpu as pltpu
from jax.sharding import PartitionSpec as P

D = 2048
HEAD_DIM = 128
CAP = 16


def per_device(
    queries,
    keys,
    values,
    out_weight,
    residual_in,
    gate_weight,
    up_weight,
    down_weight,
    expert_ids,
    route_gates,
):
    scale = HEAD_DIM ** (-0.5)
    local_tokens = queries.shape[0]
    head_count = queries.shape[1] // HEAD_DIM
    query_heads = queries.reshape(local_tokens, head_count, HEAD_DIM)
    key_piece = lax.all_gather(keys, "ctx", axis=0, tiled=True)
    value_piece = lax.all_gather(values, "ctx", axis=0, tiled=True)
    count = key_piece.shape[0]
    key_heads = key_piece.reshape(count, head_count, HEAD_DIM)
    value_heads = value_piece.reshape(count, head_count, HEAD_DIM)
    running_max = jnp.full((head_count, local_tokens), -1e30, jnp.float32)
    scores = (
        jnp.einsum("qhd,khd->hqk", query_heads, key_heads, preferred_element_type=jnp.float32)
        * scale
    )
    newest_max = jnp.maximum(running_max, jnp.max(scores, axis=2))
    weights = jnp.exp(scores - newest_max[:, :, None])
    numerator = jnp.einsum(
        "hqk,khd->hqd",
        weights.astype(jnp.bfloat16),
        value_heads,
        preferred_element_type=jnp.float32,
    )
    denominator = jnp.sum(weights, axis=2)
    final_max, numerator, denominator = (newest_max, numerator, denominator)
    attention = (numerator / denominator[:, :, None]).astype(jnp.bfloat16)
    attention = jnp.transpose(attention, (1, 0, 2)).reshape(local_tokens, head_count * HEAD_DIM)
    own_rows = residual_in.shape[0]
    hidden = residual_in.astype(jnp.float32) + lax.psum_scatter(
        jnp.dot(attention, out_weight, preferred_element_type=jnp.float32).astype(jnp.bfloat16),
        "exp",
        scatter_dimension=0,
        tiled=True,
    ).astype(jnp.float32)
    normed = (hidden * lax.rsqrt(jnp.mean(hidden * hidden, axis=1, keepdims=True) + 1e-06)).astype(
        jnp.bfloat16
    )
    owners = lax.axis_size("exp")
    flat_ids = expert_ids.reshape(-1)
    one_hot = (flat_ids[:, None] == jnp.arange(owners, dtype=jnp.int32)[None, :]).astype(jnp.int32)
    earlier = jnp.cumsum(one_hot, axis=0) - one_hot
    slot_index = jnp.sum(earlier * one_hot, axis=1)
    target = flat_ids * CAP + slot_index
    dispatch_table = (target[None, :] == jnp.arange(owners * CAP, dtype=jnp.int32)[:, None]).astype(
        jnp.bfloat16
    )
    routed = jnp.repeat(normed, 2, axis=0)
    outgoing = jnp.dot(dispatch_table, routed, preferred_element_type=jnp.float32).astype(
        jnp.bfloat16
    )
    incoming = lax.all_to_all(
        outgoing.reshape(owners, CAP, D), "exp", split_axis=0, concat_axis=0, tiled=True
    )
    slot_rows = incoming.reshape(owners * CAP, D)
    gate_part = jnp.dot(
        slot_rows,
        lax.all_gather(gate_weight[0], "ctx", axis=0, tiled=True),
        preferred_element_type=jnp.float32,
    )
    up_part = jnp.dot(
        slot_rows,
        lax.all_gather(up_weight[0], "ctx", axis=0, tiled=True),
        preferred_element_type=jnp.float32,
    )
    activation = (jax.nn.silu(gate_part) * up_part).astype(jnp.bfloat16)
    expert_result = jnp.dot(
        activation,
        lax.all_gather(down_weight[0], "ctx", axis=1, tiled=True),
        preferred_element_type=jnp.float32,
    ).astype(jnp.bfloat16)
    returned = lax.all_to_all(
        expert_result.reshape(owners, CAP, D), "exp", split_axis=0, concat_axis=0, tiled=True
    )
    per_route = jnp.einsum(
        "sr,sd->rd",
        dispatch_table,
        returned.reshape(owners * CAP, D),
        preferred_element_type=jnp.float32,
    )
    per_route = per_route.reshape(own_rows, 2, D)
    combined = per_route[:, 0, :] * route_gates[:, 0:1] + per_route[:, 1, :] * route_gates[:, 1:2]
    return (hidden + combined).astype(jnp.bfloat16)


F32 = jnp.float32
BF16 = jnp.bfloat16
HALF = D // 2


def dot(a, b):
    return jnp.dot(a, b, preferred_element_type=F32)


def block_kernel(
    owners,
    q_hbm,
    k_hbm,
    v_hbm,
    wo_hbm,
    res_hbm,
    wg_hbm,
    wu_hbm,
    wd_hbm,
    ids_hbm,
    gates_hbm,
    out_ref,
    k_ref,
    v_ref,
    res_ref,
    ids_ref,
    gates_ref,
    wo,
    wg,
    wu,
    wd,
    k_other,
    v_other,
    q_sorted,
    attn,
    mate_out,
    mate_in,
    own_part,
    reduce_out,
    reduce_in,
    hidden,
    normed_halves,
    outgoing,
    slab,
    part_out,
    part_in,
    act_own,
    act_other,
    results,
    returned,
    load_sem,
    q_sem,
    kv_send,
    kv_recv,
    mate_send,
    mate_recv,
    red_send,
    red_recv,
    disp_send,
    disp_recv,
    part_send,
    part_recv,
    act_send,
    act_recv,
    ret_send,
    ret_recv,
):
    chips = owners // 2
    ctx = lax.axis_index("ctx")
    exp = lax.axis_index("exp")
    chip, core = exp // 2, lax.rem(exp, 2)
    rows = res_ref.shape[0]
    slots = owners * CAP
    group_rows = chips * rows
    other_ctx = 1 - ctx

    def place(dc, de):
        return {
            "ctx": other_ctx if dc else ctx,
            "exp": lax.rem(exp + de, owners) if de else exp,
        }

    def dot_t(a, b):
        return lax.dot_general(a, b, (((1,), (1,)), ((), ())), preferred_element_type=F32)

    def remote(src, dst, send, recv, where):
        copy = pltpu.make_async_remote_copy(
            src_ref=src,
            dst_ref=dst,
            send_sem=send,
            recv_sem=recv,
            device_id=where,
            device_id_type=pl.DeviceIdType.MESH,
        )
        copy.start()
        return copy

    def load(n, src, dst):
        copy = pltpu.make_async_copy(src, dst, load_sem.at[n])
        copy.start()
        return copy

    q_loads = []
    for n in range(owners):
        keeper = core if n >= chips else 1 - core
        start = pl.multiple_of((2 * (n % chips) + keeper) * rows, rows)
        copy = pltpu.make_async_copy(
            q_hbm.at[pl.ds(start, rows), :], q_sorted.at[pl.ds(n * rows, rows), :], q_sem.at[n]
        )
        copy.start()
        q_loads.append(copy)
    k_load = load(0, k_hbm, k_ref)
    v_load = load(1, v_hbm, v_ref)
    ids_load = load(2, ids_hbm, ids_ref)
    gates_load = load(3, gates_hbm, gates_ref)
    wo_load = load(4, wo_hbm, wo)
    res_load = load(5, res_hbm, res_ref)
    partners = [(dc, de) for dc in range(2) for de in range(owners) if dc or de]
    barrier = pltpu.get_barrier_semaphore()
    for dc, de in partners:
        pl.semaphore_signal(
            barrier, inc=1, device_id=place(dc, de), device_id_type=pl.DeviceIdType.MESH
        )
    pl.semaphore_wait(barrier, len(partners))

    across = place(1, 0)
    k_copy = remote(k_hbm, k_other, kv_send.at[0], kv_recv.at[0], across)
    v_copy = remote(v_hbm, v_other, kv_send.at[1], kv_recv.at[1], across)
    wg_load = load(6, wg_hbm, wg)
    wu_load = load(7, wu_hbm, wu)
    wd_load = load(8, wd_hbm, wd)

    ids_load.wait()
    gates_load.wait()
    line = lax.broadcasted_iota(jnp.int32, (slots, rows), 0)
    picks = []
    for k in range(2):
        rel = ids_ref[k : k + 1, :] - exp
        picks.append(jnp.where(rel < 0, rel + owners, rel))
    named = [jnp.where(line == rel, 1.0, 0.0) for rel in picks]
    down_row = lax.broadcasted_iota(jnp.int32, (rows, rows), 0)
    down_col = lax.broadcasted_iota(jnp.int32, (rows, rows), 1)
    before = jnp.where(down_row < down_col, 1.0, 0.0)
    same = jnp.where(down_row == down_col, 1.0, 0.0)
    earlier = dot((named[0] + named[1]).astype(BF16), before.astype(BF16))
    tables = []
    for k in range(2):
        slot = jnp.sum(earlier * named[k], axis=0, keepdims=True)
        target = picks[k].astype(F32) * CAP + slot
        tables.append(jnp.where(line.astype(F32) == target, 1.0, 0.0))
    dispatch_t = (tables[0] + tables[1]).astype(BF16)
    combine = jnp.concatenate([table.T for table in tables], 0).astype(BF16)
    gate_columns = [
        jnp.sum(same * gates_ref[k : k + 1, :], axis=1, keepdims=True) for k in range(2)
    ]

    scale = HEAD_DIM ** (-0.5)
    head_count = q_sorted.shape[1] // HEAD_DIM

    def scores_of(h, keys):
        cols = pl.ds(h * HEAD_DIM, HEAD_DIM)
        return dot_t(q_sorted[:, cols], keys[:, cols]) * scale

    for copy in q_loads:
        copy.wait()
    k_load.wait()
    v_load.wait()
    wo_load.wait()
    near_scores = [scores_of(h, k_ref) for h in range(head_count)]
    near_tops = [jnp.max(near, axis=1, keepdims=True) for near in near_scores]
    k_copy.wait_recv()
    softmax = []
    for h in range(head_count):
        far = scores_of(h, k_other)
        top = jnp.maximum(near_tops[h], jnp.max(far, axis=1, keepdims=True))
        near, far = jnp.exp(near_scores[h] - top), jnp.exp(far - top)
        total = jnp.sum(near, axis=1, keepdims=True) + jnp.sum(far, axis=1, keepdims=True)
        cols = pl.ds(h * HEAD_DIM, HEAD_DIM)
        softmax.append((dot(near.astype(BF16), v_ref[:, cols]), far.astype(BF16), total))
    v_copy.wait_recv()
    for h in range(head_count):
        cols = pl.ds(h * HEAD_DIM, HEAD_DIM)
        numerator, far, total = softmax[h]
        attn[:, cols] = ((numerator + dot(far, v_other[:, cols])) / total).astype(BF16)

    mate = {"ctx": ctx, "exp": exp + 1 - 2 * core}
    mate_copies = []
    for c in range(2):
        mate_out[c] = dot(attn[:group_rows, :], wo[:, c * HALF : (c + 1) * HALF]).astype(BF16)
        mate_copies.append(
            remote(mate_out.at[c], mate_in.at[c], mate_send.at[c], mate_recv.at[c], mate)
        )
    red_copies = []
    own_start = pl.multiple_of(chip * rows, rows)
    res_load.wait()
    for c in range(2):
        cols = pl.ds(c * HALF, HALF)
        own_part[...] = dot(attn[group_rows:, :], wo[:, cols])
        mate_copies[c].wait_recv()
        for dz in range(chips - 1, 0, -1):
            to_chip = lax.rem(chip + dz, chips)
            start = pl.multiple_of(to_chip * rows, rows)
            reduce_out[c, dz - 1] = (
                own_part[pl.ds(start, rows), :] + mate_in[c, pl.ds(start, rows), :].astype(F32)
            ).astype(BF16)
            red_copies.append(
                remote(
                    reduce_out.at[c, dz - 1],
                    reduce_in.at[c, dz - 1],
                    red_send.at[c, dz - 1],
                    red_recv.at[c, dz - 1],
                    {"ctx": ctx, "exp": 2 * to_chip + core},
                )
            )
        hidden[:, cols] = (
            res_ref[:, cols].astype(F32)
            + own_part[pl.ds(own_start, rows), :]
            + mate_in[c, pl.ds(own_start, rows), :].astype(F32)
        )
    for c in range(2):
        cols = pl.ds(c * HALF, HALF)
        for copy in red_copies[c * (chips - 1) : (c + 1) * (chips - 1)]:
            copy.wait_recv()
        total = hidden[:, cols]
        for dz in range(chips - 1, 0, -1):
            total = total + reduce_in[c, dz - 1].astype(F32)
        hidden[:, cols] = total

    square = jnp.mean(hidden[...] * hidden[...], axis=1, keepdims=True)
    normed = (hidden[...] * lax.rsqrt(square + 1e-06)).astype(BF16)
    for c in range(2):
        normed_halves[c] = normed[:, c * HALF : (c + 1) * HALF]
    disp_copies = {}
    for dc in (1, 0):
        c = other_ctx if dc else ctx
        outgoing[dc] = dot(dispatch_t, normed_halves[c]).astype(BF16).reshape(owners, CAP, HALF)
        for de in sorted(range(owners), key=lambda e: abs(e - owners // 2)):
            if dc or de:
                disp_copies[dc, de] = remote(
                    outgoing.at[dc, de],
                    slab.at[dc, de],
                    disp_send.at[dc, de],
                    disp_recv.at[dc, de],
                    place(dc, de),
                )
    slab[0, 0] = outgoing[0, 0]
    for de in range(owners):
        disp_copies[1, de].wait_recv()
    wg_load.wait()
    wu_load.wait()
    far_rows = slab[1].reshape(slots, HALF)
    part_copies = []
    for n, weight in enumerate((wg, wu)):
        part_out[n] = dot_t(far_rows, weight[...]).astype(BF16)
        part_copies.append(
            remote(part_out.at[n], part_in.at[n], part_send.at[n], part_recv.at[n], across)
        )
    for de in range(1, owners):
        disp_copies[0, de].wait_recv()
    near_rows = slab[0].reshape(slots, HALF)
    gate_part = dot_t(near_rows, wg[...])
    up_part = dot_t(near_rows, wu[...])
    part_copies[0].wait_recv()
    gate_part = gate_part + part_in[0].astype(F32)
    gate_part = gate_part / (1.0 + jnp.exp(-gate_part))
    part_copies[1].wait_recv()
    act_own[...] = (gate_part * (up_part + part_in[1].astype(F32))).astype(BF16)
    act_copy = remote(act_own, act_other, act_send, act_recv, across)
    wd_load.wait()
    ret_copies = {}
    for dc in range(2):
        if dc:
            act_copy.wait_recv()
        result = dot((act_other if dc else act_own)[...], wd[...]).astype(BF16)
        results[dc] = result.reshape(owners, CAP, HALF)
        for de in sorted(range(owners), key=lambda e: abs(e - owners // 2)):
            if dc or de:
                ret_copies[dc, de] = remote(
                    results.at[dc, de],
                    returned.at[dc, de],
                    ret_send.at[dc, de],
                    ret_recv.at[dc, de],
                    place(dc, owners - de if de else 0),
                )
    returned[0, 0] = results[0, 0]
    for dc in range(2):
        for de in range(owners):
            if dc or de:
                ret_copies[dc, de].wait_recv()
        per_route = dot(combine, returned[dc].reshape(slots, HALF))
        cols = pl.ds(pl.multiple_of((other_ctx if dc else ctx) * HALF, HALF), HALF)
        out_ref[:, cols] = (
            hidden[:, cols]
            + per_route[:rows] * gate_columns[0]
            + per_route[rows:] * gate_columns[1]
        ).astype(BF16)

    for copy in (
        [k_copy, v_copy, act_copy]
        + mate_copies
        + red_copies
        + part_copies
        + list(disp_copies.values())
        + list(ret_copies.values())
    ):
        copy.wait_send()


def per_device_pair(
    owners,
    queries,
    keys,
    values,
    out_weight,
    residual_in,
    gate_weight,
    up_weight,
    down_weight,
    expert_ids,
    route_gates,
):
    tokens, width = queries.shape
    rows = residual_in.shape[0]
    units = gate_weight.shape[2]
    chips, slots = owners // 2, owners * CAP
    in_vmem = pl.BlockSpec(memory_space=pltpu.VMEM)
    dma = pltpu.SemaphoreType.DMA
    return pl.pallas_call(
        functools.partial(block_kernel, owners),
        out_shape=jax.ShapeDtypeStruct((rows, D), BF16),
        in_specs=[pl.BlockSpec(memory_space=pltpu.HBM)] * 10,
        out_specs=in_vmem,
        scratch_shapes=[
            pltpu.VMEM((tokens, width), BF16),
            pltpu.VMEM((tokens, width), BF16),
            pltpu.VMEM((rows, D), BF16),
            pltpu.VMEM((2, rows), jnp.int32),
            pltpu.VMEM((2, rows), F32),
            pltpu.VMEM((width, D), BF16),
            pltpu.VMEM((units, HALF), BF16),
            pltpu.VMEM((units, HALF), BF16),
            pltpu.VMEM((units, HALF), BF16),
            pltpu.VMEM((tokens, width), BF16),
            pltpu.VMEM((tokens, width), BF16),
            pltpu.VMEM((tokens, width), BF16),
            pltpu.VMEM((tokens, width), BF16),
            pltpu.VMEM((2, chips * rows, HALF), BF16),
            pltpu.VMEM((2, chips * rows, HALF), BF16),
            pltpu.VMEM((chips * rows, HALF), F32),
            pltpu.VMEM((2, chips - 1, rows, HALF), BF16),
            pltpu.VMEM((2, chips - 1, rows, HALF), BF16),
            pltpu.VMEM((rows, D), F32),
            pltpu.VMEM((2, rows, HALF), BF16),
            pltpu.VMEM((2, owners, CAP, HALF), BF16),
            pltpu.VMEM((2, owners, CAP, HALF), BF16),
            pltpu.VMEM((2, slots, units), BF16),
            pltpu.VMEM((2, slots, units), BF16),
            pltpu.VMEM((slots, units), BF16),
            pltpu.VMEM((slots, units), BF16),
            pltpu.VMEM((2, owners, CAP, HALF), BF16),
            pltpu.VMEM((2, owners, CAP, HALF), BF16),
            dma((9,)),
            dma((owners,)),
            dma((2,)),
            dma((2,)),
            dma((2,)),
            dma((2,)),
            dma((2, chips - 1)),
            dma((2, chips - 1)),
            dma((2, owners)),
            dma((2, owners)),
            dma((2,)),
            dma((2,)),
            dma,
            dma,
            dma((2, owners)),
            dma((2, owners)),
        ],
        compiler_params=pltpu.CompilerParams(
            collective_id=0, has_side_effects=True, vmem_limit_bytes=64 * 1024 * 1024
        ),
    )(
        queries,
        keys,
        values,
        out_weight,
        residual_in,
        gate_weight[0].T,
        up_weight[0].T,
        down_weight[0],
        expert_ids.T,
        route_gates.T,
    )


def solution(mesh):
    if mesh.shape["ctx"] == 2 and mesh.shape["exp"] % 2 == 0:
        body = functools.partial(per_device_pair, mesh.shape["exp"])
    else:
        body = per_device
    return jax.shard_map(
        body,
        mesh=mesh,
        in_specs=(
            P(("group", "ctx"), "exp"),
            P(("group", "ctx"), "exp"),
            P(("group", "ctx"), "exp"),
            P("exp", None),
            P(("group", "ctx", "exp"), None),
            P("exp", "ctx", None),
            P("exp", "ctx", None),
            P("exp", None, "ctx"),
            P(("group", "ctx", "exp"), None),
            P(("group", "ctx", "exp"), None),
        ),
        out_specs=P(("group", "ctx", "exp"), None),
        check_vma=False,
    )
```
